32 devices in a mesh: lat: 8 (over z, x), lon: 4 (over y, core).
Axes of the slice: x: 2, y: 2, z: 4, core: 2. Of those that a mesh axis runs over, the one named last changes fastest.
Arguments:
- nodes: bfloat16 [8192, 256], P(('lat', 'lon')), may hold values from -6 to 6
- edges: bfloat16 [98304, 256], P(('lat', 'lon')), may hold values from -6 to 6
- senders: int32 [98304], P(('lat', 'lon')), may hold values from 0 to 767, as said below
- receivers: int32 [98304], P(('lat', 'lon')), may hold values from 0 to 255
- edge_count: int32 [32], P(('lat', 'lon')), may hold values from 1536 to 3072, as said below
- send_index: int32 [128, 64], P(('lat', 'lon')), may hold values from 0 to 255
- rim_index: int32 [64, 128], P(('lat', 'lon')), may hold values from 0 to 255
- edge_w1: bfloat16 [768, 256], replicated, may hold values from -0.21875 to 0.21875
- edge_b1: float32 [256], replicated, may hold values from -3 to 3
- edge_w2: bfloat16 [256, 256], replicated, may hold values from -0.375 to 0.375
- edge_gain: float32 [256], replicated, may hold values from 0.1 to 1.9
- node_w1: bfloat16 [512, 256], replicated, may hold values from -0.25 to 0.25
- node_b1: float32 [256], replicated, may hold values from -3 to 3
- node_w2: bfloat16 [256, 256], replicated, may hold values from -0.375 to 0.375
- node_gain: float32 [256], replicated, may hold values from 0.1 to 1.9
Outputs:
- new_nodes: bfloat16 [8192, 256], P(('lat', 'lon'))
- new_edges: bfloat16 [98304, 256], P(('lat', 'lon'))
The draws below stay inside these ranges and needn't reach their ends.
Inputs may be any that keep to these rules, and one draw needn't show every extreme that they name: `senders`: A sender in the first band never names the slots of the band before it, one in the last band never those of the band after it. `edge_count`: some device has all 3072 slots live.
All inputs are finite; a program needn't handle non-finite values.
Results may differ from the reference program's by a relative error of at most 0.009.
Values may be sent and summed in bfloat16 or wider, within the bound.
A program may use at most 64 MiB of HBM per device.

```python
import jax
import jax.numpy as jnp
from jax import lax

D = 256
NODE_DEV = 256
EDGE_DEV = 3072
HALO = 64
RIM = 128
DEVICES_ALL = 32
NODES = 8192
EDGES = 98304
TABLE = 768
N_LAT = 8
N_LON = 4


def draw_senders(key, part):
    key = jax.random.fold_in(key, 5)
    keys = jax.random.split(key, 5)
    kind = jax.random.randint(keys[0], (EDGES,), 0, 10)
    local = jax.random.randint(keys[1], (EDGES,), 0, NODE_DEV)
    listed = NODE_DEV + jax.random.randint(keys[2], (EDGES,), 0, N_LON * HALO)
    offset = jax.random.randint(keys[3], (EDGES,), 0, RIM)
    side = jax.random.randint(keys[4], (EDGES,), 0, 2)
    band = jnp.arange(EDGES, dtype=jnp.int32) // EDGE_DEV // N_LON
    side = jnp.where(band == 0, 1, jnp.where(band == N_LAT - 1, 0, side))
    rim = NODE_DEV + N_LON * HALO + side * RIM + offset
    return jnp.where(kind < 6, local, jnp.where(kind < 9, listed, rim)).astype(jnp.int32)


def draw_edge_count(key, part):
    key = jax.random.fold_in(key, 9)
    keys = jax.random.split(key, 3)
    counts = jax.random.randint(keys[0], (N_LAT * N_LON,), EDGE_DEV // 2, EDGE_DEV + 1)
    fullest = jax.random.randint(keys[1], (), 0, N_LAT * N_LON)
    counts = counts.at[fullest].set(EDGE_DEV)
    emptiest = (fullest + 1 + jax.random.randint(keys[2], (), 0, N_LAT * N_LON - 1)) % (N_LAT * N_LON)
    return counts.at[emptiest].set(EDGE_DEV // 2).astype(jnp.int32)


def place_ends(array, own_key, low, high):
    shape = array.shape
    spot = [jax.random.randint(jax.random.fold_in(own_key, axis), (), 0, shape[axis]) for axis in range(len(shape))]
    array = array.at[tuple(spot)].set(low)
    longest = shape.index(max(shape))
    spot[longest] = (spot[longest] + 1) % shape[longest]
    return array.at[tuple(spot)].set(high)


def shard_levels(rng, dims, cuts, smallest, largest):
    def one(position, blocks):
        steps = jax.random.uniform(jax.random.fold_in(jax.random.fold_in(rng, 6), position), (blocks,), jnp.float32, smallest / len(cuts), largest / len(cuts))
        return jnp.repeat(jnp.exp(steps), dims[position] // blocks).reshape((-1,) + (1,) * (len(dims) - position - 1))

    loudness = one(*cuts[0])
    for cut in cuts[1:]:
        loudness = loudness * one(*cut)
    return loudness


def scatter_about(own_key, dims, scale, limit, cuts=(), kind=jnp.bfloat16):
    drawn = scale * jax.random.normal(own_key, dims, jnp.float32)
    if cuts:
        drawn = drawn * shard_levels(own_key, dims, cuts, -0.22, 0.18)
    return jnp.clip(drawn, -limit, limit).astype(kind)


def setup_inputs(seed: int = 0) -> dict:
    arg_keys = jax.random.split(jax.random.key(seed), 16)
    nodes = scatter_about(arg_keys[0], (NODES, D), 1.0, 6.0, ((0, 32),))
    edges = scatter_about(arg_keys[1], (EDGES, D), 1.0, 6.0, ((0, 32),))
    senders = draw_senders(jax.random.fold_in(arg_keys[15], 71), 0)
    receivers = place_ends(jax.random.randint(arg_keys[3], (EDGES,), 0, NODE_DEV), jax.random.fold_in(arg_keys[3], 1), 0, NODE_DEV - 1).astype(jnp.int32)
    edge_count = draw_edge_count(jax.random.fold_in(arg_keys[15], 71), 0)
    send_index = place_ends(jax.random.randint(arg_keys[5], (DEVICES_ALL * N_LON, HALO), 0, NODE_DEV), jax.random.fold_in(arg_keys[5], 1), 0, NODE_DEV - 1).astype(jnp.int32)
    rim_index = place_ends(jax.random.randint(arg_keys[6], (DEVICES_ALL * 2, RIM), 0, NODE_DEV), jax.random.fold_in(arg_keys[6], 1), 0, NODE_DEV - 1).astype(jnp.int32)
    edge_w1 = scatter_about(arg_keys[7], (3 * D, D), (3 * D) ** -0.5, 0.21875)
    edge_b1 = scatter_about(arg_keys[8], (D,), 0.5, 3.0, (), jnp.float32)
    edge_w2 = scatter_about(arg_keys[9], (D, D), D ** -0.5, 0.375)
    edge_gain = jnp.clip(1.0 + 0.18 * jax.random.normal(arg_keys[10], (D,), jnp.float32), 0.1, 1.9)
    node_w1 = scatter_about(arg_keys[11], (2 * D, D), (2 * D) ** -0.5, 0.25)
    node_b1 = scatter_about(arg_keys[12], (D,), 0.5, 3.0, (), jnp.float32)
    node_w2 = scatter_about(arg_keys[13], (D, D), D ** -0.5, 0.375)
    node_gain = jnp.clip(1.0 + 0.18 * jax.random.normal(arg_keys[14], (D,), jnp.float32), 0.1, 1.9)
    return {"nodes": nodes, "edges": edges, "senders": senders, "receivers": receivers, "edge_count": edge_count, "send_index": send_index, "rim_index": rim_index, "edge_w1": edge_w1, "edge_b1": edge_b1, "edge_w2": edge_w2, "edge_gain": edge_gain, "node_w1": node_w1, "node_b1": node_b1, "node_w2": node_w2, "node_gain": node_gain}


def layer_norm(values, gain):
    mean = lax.optimization_barrier(jnp.mean(values, axis=-1, keepdims=True))
    centred = values - mean
    var = lax.optimization_barrier(jnp.mean(centred * centred, axis=-1, keepdims=True))
    return centred * lax.rsqrt(var + 1e-05) * gain

def build_tables(nodes, send_index, rim_index):
    grid = nodes.reshape(N_LAT, N_LON, NODE_DEV, D)
    lists = send_index.reshape(N_LAT, N_LON, N_LON * HALO)
    picked = jnp.take_along_axis(grid, lists[..., None], axis=2)
    picked = picked.reshape(N_LAT, N_LON, N_LON, HALO, D).transpose(0, 2, 1, 3, 4)
    picked = picked.reshape(N_LAT, N_LON, N_LON * HALO, D)
    rims = rim_index.reshape(N_LAT, N_LON, 2, RIM)
    upward = jnp.take_along_axis(grid, rims[:, :, 0][..., None], axis=2)
    downward = jnp.take_along_axis(grid, rims[:, :, 1][..., None], axis=2)
    blank = jnp.zeros((1, N_LON, RIM, D), jnp.bfloat16)
    from_below = jnp.concatenate([blank, upward[:-1]], axis=0)
    from_above = jnp.concatenate([downward[1:], blank], axis=0)
    table = jnp.concatenate([grid, picked, from_below, from_above], axis=2)
    return table.reshape(N_LAT * N_LON, TABLE, D)

def device_step(items, weights):
    table, edge, sender, receiver, count = items
    edge_w1, edge_b1, edge_w2, edge_gain, node_w1, node_b1, node_w2, node_gain = weights
    local = table[:NODE_DEV]
    pre = jnp.dot(edge, edge_w1[:D], preferred_element_type=jnp.float32)
    pre = pre + jnp.dot(table[sender], edge_w1[D:2 * D], preferred_element_type=jnp.float32)
    pre = pre + jnp.dot(local[receiver], edge_w1[2 * D:], preferred_element_type=jnp.float32)
    hidden = jax.nn.silu(pre + edge_b1).astype(jnp.bfloat16)
    update = layer_norm(jnp.dot(hidden, edge_w2, preferred_element_type=jnp.float32), edge_gain)
    live = jnp.arange(EDGE_DEV, dtype=jnp.int32) < count
    update = jnp.where(live[:, None], update, 0.0).astype(jnp.bfloat16)
    new_edge = (edge.astype(jnp.float32) + update.astype(jnp.float32)).astype(jnp.bfloat16)
    messages = jax.ops.segment_sum(update.astype(jnp.float32), receiver, NODE_DEV).astype(jnp.bfloat16)
    node_pre = jnp.dot(local, node_w1[:D], preferred_element_type=jnp.float32)
    node_pre = node_pre + jnp.dot(messages, node_w1[D:], preferred_element_type=jnp.float32)
    node_hidden = jax.nn.silu(node_pre + node_b1).astype(jnp.bfloat16)
    node_out = layer_norm(jnp.dot(node_hidden, node_w2, preferred_element_type=jnp.float32), node_gain)
    new_node = (local.astype(jnp.float32) + node_out).astype(jnp.bfloat16)
    return (new_node, new_edge)

def reference(nodes, edges, senders, receivers, edge_count, send_index, rim_index, edge_w1, edge_b1, edge_w2, edge_gain, node_w1, node_b1, node_w2, node_gain):
    tables = build_tables(nodes, send_index, rim_index)
    weights = (edge_w1, edge_b1, edge_w2, edge_gain, node_w1, node_b1, node_w2, node_gain)
    items = (tables, edges.reshape(-1, EDGE_DEV, D), senders.reshape(-1, EDGE_DEV), receivers.reshape(-1, EDGE_DEV), edge_count)
    new_nodes, new_edges = lax.map(lambda item: device_step(item, weights), items)
    return (new_nodes.reshape(NODES, D), new_edges.reshape(EDGES, D))
```

```python
import functools

import jax
import jax.numpy as jnp
from jax import lax
from jax.experimental import pallas as pl
from jax.experimental.pallas import tpu as pltpu
from jax.sharding import PartitionSpec as P

BF16 = jnp.bfloat16
F32 = jnp.float32
MESH = pl.DeviceIdType.MESH
LANES = 128
CHUNK = 512
AHEAD = 6


def dot(a, b):
    return jnp.dot(a, b, preferred_element_type=F32)


def lane_ids(rows):
    return lax.broadcasted_iota(jnp.int32, (rows, LANES), 1).astype(jnp.int16)


def row_ids(rows):
    return lax.broadcasted_iota(jnp.int32, (rows, LANES), 0).astype(jnp.int16)


def mark(hit):
    return jnp.where(hit, jnp.ones(hit.shape, BF16), jnp.zeros(hit.shape, BF16))


def pick_rows(columns, low, high):
    n = columns.shape[0]
    spread = jnp.broadcast_to(columns, (n, LANES)).astype(jnp.int16)
    lanes = lane_ids(n)
    tiles = [mark(spread == lanes + jnp.int16(t)) for t in range(low, high, LANES)]
    return jnp.concatenate(tiles, axis=1)


def turned(block):
    short = LANES - block.shape[0]
    if short:
        block = jnp.concatenate([block, jnp.zeros((short, LANES), jnp.int32)], axis=0)
    return jnp.transpose(block)


def centred_weights(w):
    w = w.astype(F32)
    return (w - jnp.mean(w, axis=-1, keepdims=True)).astype(BF16)


def halved_silu(h):
    return (h + h * jnp.tanh(h)).astype(BF16)


def inverse_spread(y, ones):
    return lax.rsqrt(dot((y * y).astype(BF16), ones) + 1e-05)


def kernel(
    n_lat,
    n_lon,
    count,
    senders,
    receivers,
    send_index,
    rim_index,
    b1,
    gain,
    c1,
    ngain,
    nodes_in,
    edges_in,
    w1_in,
    w2_in,
    v1_in,
    v2_in,
    new_nodes,
    new_edges,
    nodes,
    edges,
    w1,
    w2,
    v1,
    v2,
    table,
    outgoing,
    pre,
    fresh,
    fresh_nodes,
    load_sem,
    edge_sem,
    store_sem,
    send_sem,
    recv_sem,
):
    a, b = lax.axis_index("lat"), lax.axis_index("lon")
    node_rows, width = nodes.shape
    edge_rows = edges.shape[0]
    halo = send_index.shape[1]
    rim = rim_index.shape[1]
    rows = table.shape[0]
    halo_at, rim_at = node_rows, node_rows + n_lon * halo
    chunks = edge_rows // CHUNK
    blocks = CHUNK // LANES

    barrier = pltpu.get_barrier_semaphore()
    for d in range(1, n_lon):
        pl.semaphore_signal(
            barrier, inc=1, device_id=(a, lax.rem(b + d, n_lon)), device_id_type=MESH
        )

    @pl.when(a > 0)
    def _():
        pl.semaphore_signal(barrier, inc=1, device_id=(a - 1, b), device_id_type=MESH)

    @pl.when(a < n_lat - 1)
    def _():
        pl.semaphore_signal(barrier, inc=1, device_id=(a + 1, b), device_id_type=MESH)

    loads = [
        pltpu.make_async_copy(src, dst, load_sem.at[i])
        for i, (src, dst) in enumerate(
            [(nodes_in, nodes), (w1_in, w1), (w2_in, w2), (v1_in, v1), (v2_in, v2)]
        )
    ]
    edge_loads = [
        pltpu.make_async_copy(
            edges_in.at[pl.ds(i * CHUNK, CHUNK)], edges.at[pl.ds(i * CHUNK, CHUNK)], edge_sem.at[i]
        )
        for i in range(chunks)
    ]
    loads[0].start()
    loads[1].start()
    for copy in edge_loads:
        copy.start()
    for copy in loads[2:]:
        copy.start()

    lists = jnp.concatenate(
        [send_index[...], jnp.zeros((n_lon, LANES - halo), jnp.int32)], axis=1
    )
    list_turned = turned(jnp.concatenate([rim_index[...], lists], axis=0))
    sender_turned = turned(senders[...])
    receiver_turned = turned(receivers[...])

    loads[0].wait()
    loads[1].wait()
    own = nodes[...]
    table[:node_rows] = (0.5 * dot(own, w1[width : 2 * width])).astype(BF16)
    for p in range(n_lon):
        chosen = pick_rows(list_turned[:halo, 2 + p : 3 + p], 0, node_rows)
        outgoing[p * halo : (p + 1) * halo] = dot(chosen, table[:node_rows]).astype(BF16)
    for side in range(2):
        chosen = pick_rows(list_turned[:, side : side + 1], 0, node_rows)
        at = n_lon * halo + side * rim
        outgoing[at : at + rim] = dot(chosen, table[:node_rows]).astype(BF16)
    mine = pl.multiple_of(b * halo, halo)
    table[pl.ds(halo_at + mine, halo)] = outgoing[pl.ds(mine, halo)]

    @pl.when(a == 0)
    def _():
        table[rim_at : rim_at + rim] = jnp.zeros((rim, width), BF16)

    @pl.when(a == n_lat - 1)
    def _():
        table[rim_at + rim :] = jnp.zeros((rim, width), BF16)

    below = jnp.where(a > 0, 1, 0)
    above = jnp.where(a < n_lat - 1, 1, 0)
    pl.semaphore_wait(barrier, n_lon - 1 + below + above)
    band = []
    for d in range(1, n_lon):
        p = lax.rem(b + d, n_lon)
        copy = pltpu.make_async_remote_copy(
            src_ref=outgoing.at[pl.ds(pl.multiple_of(p * halo, halo), halo)],
            dst_ref=table.at[pl.ds(halo_at + mine, halo)],
            send_sem=send_sem.at[d - 1],
            recv_sem=recv_sem.at[d - 1],
            device_id=(a, p),
            device_id_type=MESH,
        )
        copy.start()
        band.append(copy)
    rims = [
        pltpu.make_async_remote_copy(
            src_ref=outgoing.at[pl.ds(n_lon * halo + side * rim, rim)],
            dst_ref=table.at[pl.ds(rim_at + side * rim, rim)],
            send_sem=send_sem.at[n_lon - 1 + side],
            recv_sem=recv_sem.at[n_lon - 1 + side],
            device_id=(a + 1 - 2 * side, b),
            device_id_type=MESH,
        )
        for side in range(2)
    ]

    @pl.when(a < n_lat - 1)
    def _():
        rims[0].start()

    @pl.when(a > 0)
    def _():
        rims[1].start()

    by_receiver = (0.5 * (dot(own, w1[2 * width :]) + b1[...])).astype(BF16)
    near = jnp.concatenate(
        [(0.5 * w1[:width].astype(F32)).astype(BF16), by_receiver, table[:node_rows]], axis=0
    )

    def near_part(i):
        edge_loads[i].wait()
        marks = []
        for j in range(i * blocks, (i + 1) * blocks):
            marks.append(
                jnp.concatenate(
                    [
                        pick_rows(receiver_turned[:, j : j + 1], 0, node_rows),
                        pick_rows(sender_turned[:, j : j + 1], 0, node_rows),
                    ],
                    axis=1,
                )
            )
        marks = jnp.concatenate(marks, axis=0)
        return dot(jnp.concatenate([edges[i * CHUNK : (i + 1) * CHUNK], marks], axis=1), near)

    for i in range(min(AHEAD, chunks)):
        pre[i * CHUNK : (i + 1) * CHUNK] = near_part(i)
    for copy in loads[2:]:
        copy.wait()
    w2c = centred_weights(w2[...])
    v2c = centred_weights(v2[...])
    ones = jnp.full((width, LANES), 1.0 / width, BF16)
    node_pre = dot(own, v1[:width]) + c1[...]

    for copy in band:
        copy.wait_recv()

    @pl.when(a > 0)
    def _():
        rims[0].wait_recv()

    @pl.when(a < n_lat - 1)
    def _():
        rims[1].wait_recv()

    far = table[node_rows:]
    live = count[0]
    messages = jnp.zeros((node_rows, width), F32)
    stores = []
    for i in range(chunks):
        span = slice(i * CHUNK, (i + 1) * CHUNK)
        marks = jnp.concatenate(
            [
                pick_rows(sender_turned[:, j : j + 1], node_rows, rows)
                for j in range(i * blocks, (i + 1) * blocks)
            ],
            axis=0,
        )
        start = pre[span] if i < AHEAD else near_part(i)
        hidden = halved_silu(start + dot(marks, far))
        y = dot(hidden, w2c)
        scale = inverse_spread(y, ones)
        slot = lax.broadcasted_iota(jnp.int32, scale.shape, 0) + i * CHUNK
        scale = jnp.where(slot < live, scale, 0.0)
        scale = jnp.concatenate([scale] * (width // LANES), axis=1)
        update = (y * scale * gain[...]).astype(BF16)
        fresh[span] = edges[span] + update
        copy = pltpu.make_async_copy(fresh.at[span], new_edges.at[span], store_sem.at[i])
        copy.start()
        stores.append(copy)
        ids = row_ids(node_rows)
        member = jnp.concatenate(
            [
                mark(
                    jnp.broadcast_to(receivers[j : j + 1], (node_rows, LANES)).astype(jnp.int16)
                    == ids
                )
                for j in range(i * blocks, (i + 1) * blocks)
            ],
            axis=1,
        )
        messages = messages + dot(member, update)

    node_pre = node_pre + dot(messages.astype(BF16), v1[width:])
    z = dot(halved_silu(0.5 * node_pre), v2c)
    scale = inverse_spread(z, ones)
    scale = jnp.concatenate([scale] * (width // LANES), axis=1)
    fresh_nodes[...] = (own.astype(F32) + z * scale * ngain[...]).astype(BF16)
    copy = pltpu.make_async_copy(fresh_nodes, new_nodes, store_sem.at[chunks])
    copy.start()
    stores.append(copy)

    for copy in band:
        copy.wait_send()

    @pl.when(a < n_lat - 1)
    def _():
        rims[0].wait_send()

    @pl.when(a > 0)
    def _():
        rims[1].wait_send()

    for copy in stores:
        copy.wait()


def local(
    n_lat,
    n_lon,
    nodes,
    edges,
    senders,
    receivers,
    edge_count,
    send_index,
    rim_index,
    edge_w1,
    edge_b1,
    edge_w2,
    edge_gain,
    node_w1,
    node_b1,
    node_w2,
    node_gain,
):
    node_rows, width = nodes.shape
    edge_rows = edges.shape[0]
    halo, rim = send_index.shape[1], rim_index.shape[1]
    listed = n_lon * halo + 2 * rim
    chunks = edge_rows // CHUNK
    vmem = pl.BlockSpec(memory_space=pltpu.VMEM)
    anywhere = pl.BlockSpec(memory_space=pl.ANY)
    return pl.pallas_call(
        functools.partial(kernel, n_lat, n_lon),
        out_shape=(
            jax.ShapeDtypeStruct(nodes.shape, BF16),
            jax.ShapeDtypeStruct(edges.shape, BF16),
        ),
        in_specs=[pl.BlockSpec(memory_space=pltpu.SMEM)] + [vmem] * 8 + [anywhere] * 6,
        out_specs=(anywhere, anywhere),
        scratch_shapes=[
            pltpu.VMEM(nodes.shape, BF16),
            pltpu.VMEM(edges.shape, BF16),
            pltpu.VMEM(edge_w1.shape, BF16),
            pltpu.VMEM(edge_w2.shape, BF16),
            pltpu.VMEM(node_w1.shape, BF16),
            pltpu.VMEM(node_w2.shape, BF16),
            pltpu.VMEM((node_rows + listed, width), BF16),
            pltpu.VMEM((listed, width), BF16),
            pltpu.VMEM((edge_rows, width), F32),
            pltpu.VMEM(edges.shape, BF16),
            pltpu.VMEM(nodes.shape, BF16),
            pltpu.SemaphoreType.DMA((5,)),
            pltpu.SemaphoreType.DMA((chunks,)),
            pltpu.SemaphoreType.DMA((chunks + 1,)),
            pltpu.SemaphoreType.DMA((n_lon + 1,)),
            pltpu.SemaphoreType.DMA((n_lon + 1,)),
        ],
        compiler_params=pltpu.CompilerParams(
            collective_id=0, has_side_effects=True, vmem_limit_bytes=48 * 1024 * 1024
        ),
    )(
        edge_count,
        senders.reshape(-1, LANES),
        receivers.reshape(-1, LANES),
        send_index,
        rim_index,
        edge_b1.reshape(1, width),
        edge_gain.reshape(1, width),
        node_b1.reshape(1, width),
        node_gain.reshape(1, width),
        nodes,
        edges,
        edge_w1,
        edge_w2,
        node_w1,
        node_w2,
    )


def solution(mesh):
    rows, flat = P(("lat", "lon"), None), P(("lat", "lon"))
    return jax.shard_map(
        functools.partial(local, mesh.shape["lat"], mesh.shape["lon"]),
        mesh=mesh,
        in_specs=(rows, rows, flat, flat, flat, rows, rows) + (P(),) * 8,
        out_specs=(rows, rows),
        check_vma=False,
    )
```

```python
import functools

import jax
import jax.numpy as jnp
from jax import lax
from jax.experimental import pallas as pl
from jax.experimental.pallas import tpu as pltpu
from jax.sharding import PartitionSpec as P

BF16 = jnp.bfloat16
F32 = jnp.float32
MESH = pl.DeviceIdType.MESH
LANES = 128
CHUNK = 512
AHEAD = 6


def dot(a, b):
    return jnp.dot(a, b, preferred_element_type=F32)


def lane_ids(rows):
    return lax.broadcasted_iota(jnp.int32, (rows, LANES), 1).astype(jnp.int16)


def row_ids(rows):
    return lax.broadcasted_iota(jnp.int32, (rows, LANES), 0).astype(jnp.int16)


def mark(hit):
    return jnp.where(hit, jnp.ones(hit.shape, BF16), jnp.zeros(hit.shape, BF16))


def pick_rows(columns, low, high):
    n = columns.shape[0]
    spread = jnp.broadcast_to(columns, (n, LANES)).astype(jnp.int16)
    lanes = lane_ids(n)
    tiles = [mark(spread == lanes + jnp.int16(t)) for t in range(low, high, LANES)]
    return jnp.concatenate(tiles, axis=1)


def turned(block):
    short = LANES - block.shape[0]
    if short:
        block = jnp.concatenate([block, jnp.zeros((short, LANES), jnp.int32)], axis=0)
    return jnp.transpose(block)


def centred_weights(w):
    w = w.astype(F32)
    return (w - jnp.mean(w, axis=-1, keepdims=True)).astype(BF16)


def halved_silu(h):
    return (h + h * jnp.tanh(h)).astype(BF16)


def inverse_spread(y, ones):
    return lax.rsqrt(dot((y * y).astype(BF16), ones) + 1e-05)


def kernel(
    n_lat,
    n_lon,
    count,
    nodes_in,
    w1_in,
    send_index_in,
    rim_index_in,
    senders_in,
    receivers_in,
    b1_in,
    gain_in,
    c1_in,
    ngain_in,
    w2_in,
    v1_in,
    v2_in,
    edges_in,
    new_nodes,
    new_edges,
    nodes,
    w1,
    send_index,
    rim_index,
    senders,
    receivers,
    b1,
    gain,
    c1,
    ngain,
    w2,
    v1,
    v2,
    edges,
    table,
    outgoing,
    pre,
    fresh,
    fresh_nodes,
    load_sem,
    store_sem,
    send_sem,
    recv_sem,
):
    a, b = lax.axis_index("lat"), lax.axis_index("lon")
    node_rows, width = nodes.shape
    edge_rows = edges.shape[0]
    halo = send_index.shape[1]
    rim = rim_index.shape[1]
    rows = table.shape[0]
    halo_at, rim_at = node_rows, node_rows + n_lon * halo
    chunks = edge_rows // CHUNK
    blocks = CHUNK // LANES

    barrier = pltpu.get_barrier_semaphore()
    for d in range(1, n_lon):
        pl.semaphore_signal(
            barrier, inc=1, device_id=(a, lax.rem(b + d, n_lon)), device_id_type=MESH
        )

    @pl.when(a > 0)
    def _():
        pl.semaphore_signal(barrier, inc=1, device_id=(a - 1, b), device_id_type=MESH)

    @pl.when(a < n_lat - 1)
    def _():
        pl.semaphore_signal(barrier, inc=1, device_id=(a + 1, b), device_id_type=MESH)

    pairs = [
        (nodes_in, nodes),
        (w1_in, w1),
        (send_index_in, send_index),
        (rim_index_in, rim_index),
        (senders_in, senders),
        (receivers_in, receivers),
        (b1_in, b1),
        (gain_in, gain),
        (c1_in, c1),
        (ngain_in, ngain),
        (w2_in, w2),
        (v1_in, v1),
        (v2_in, v2),
        (edges_in, edges),
    ]
    loads = [
        pltpu.make_async_copy(src, dst, load_sem.at[i]) for i, (src, dst) in enumerate(pairs)
    ]
    for copy in loads:
        copy.start()
    for copy in loads[:4]:
        copy.wait()

    lists = jnp.concatenate(
        [send_index[...], jnp.zeros((n_lon, LANES - halo), jnp.int32)], axis=1
    )
    list_turned = turned(jnp.concatenate([rim_index[...], lists], axis=0))
    own = nodes[...]
    table[:node_rows] = (0.5 * dot(own, w1[width : 2 * width])).astype(BF16)
    for p in range(n_lon):
        chosen = pick_rows(list_turned[:halo, 2 + p : 3 + p], 0, node_rows)
        outgoing[p * halo : (p + 1) * halo] = dot(chosen, table[:node_rows]).astype(BF16)
    for side in range(2):
        chosen = pick_rows(list_turned[:, side : side + 1], 0, node_rows)
        at = n_lon * halo + side * rim
        outgoing[at : at + rim] = dot(chosen, table[:node_rows]).astype(BF16)
    mine = pl.multiple_of(b * halo, halo)
    table[pl.ds(halo_at + mine, halo)] = outgoing[pl.ds(mine, halo)]

    @pl.when(a == 0)
    def _():
        table[rim_at : rim_at + rim] = jnp.zeros((rim, width), BF16)

    @pl.when(a == n_lat - 1)
    def _():
        table[rim_at + rim :] = jnp.zeros((rim, width), BF16)

    below = jnp.where(a > 0, 1, 0)
    above = jnp.where(a < n_lat - 1, 1, 0)
    pl.semaphore_wait(barrier, n_lon - 1 + below + above)
    band = []
    for d in range(1, n_lon):
        p = lax.rem(b + d, n_lon)
        copy = pltpu.make_async_remote_copy(
            src_ref=outgoing.at[pl.ds(pl.multiple_of(p * halo, halo), halo)],
            dst_ref=table.at[pl.ds(halo_at + mine, halo)],
            send_sem=send_sem.at[d - 1],
            recv_sem=recv_sem.at[d - 1],
            device_id=(a, p),
            device_id_type=MESH,
        )
        copy.start()
        band.append(copy)
    rims = [
        pltpu.make_async_remote_copy(
            src_ref=outgoing.at[pl.ds(n_lon * halo + side * rim, rim)],
            dst_ref=table.at[pl.ds(rim_at + side * rim, rim)],
            send_sem=send_sem.at[n_lon - 1 + side],
            recv_sem=recv_sem.at[n_lon - 1 + side],
            device_id=(a + 1 - 2 * side, b),
            device_id_type=MESH,
        )
        for side in range(2)
    ]

    @pl.when(a < n_lat - 1)
    def _():
        rims[0].start()

    @pl.when(a > 0)
    def _():
        rims[1].start()

    for copy in loads[4:]:
        copy.wait()
    sender_turned = turned(senders[...])
    receiver_turned = turned(receivers[...])
    by_receiver = (0.5 * (dot(own, w1[2 * width :]) + b1[...])).astype(BF16)
    near = jnp.concatenate(
        [(0.5 * w1[:width].astype(F32)).astype(BF16), by_receiver, table[:node_rows]], axis=0
    )

    def near_part(i):
        marks = []
        for j in range(i * blocks, (i + 1) * blocks):
            marks.append(
                jnp.concatenate(
                    [
                        pick_rows(receiver_turned[:, j : j + 1], 0, node_rows),
                        pick_rows(sender_turned[:, j : j + 1], 0, node_rows),
                    ],
                    axis=1,
                )
            )
        marks = jnp.concatenate(marks, axis=0)
        return dot(jnp.concatenate([edges[i * CHUNK : (i + 1) * CHUNK], marks], axis=1), near)

    for i in range(min(AHEAD, chunks)):
        pre[i * CHUNK : (i + 1) * CHUNK] = near_part(i)
    w2c = centred_weights(w2[...])
    v2c = centred_weights(v2[...])
    ones = jnp.full((width, LANES), 1.0 / width, BF16)
    node_pre = dot(own, v1[:width]) + c1[...]

    for copy in band:
        copy.wait_recv()

    @pl.when(a > 0)
    def _():
        rims[0].wait_recv()

    @pl.when(a < n_lat - 1)
    def _():
        rims[1].wait_recv()

    far = table[node_rows:]
    live = count[0]
    messages = jnp.zeros((node_rows, width), F32)
    stores = []
    for i in range(chunks):
        span = slice(i * CHUNK, (i + 1) * CHUNK)
        marks = jnp.concatenate(
            [
                pick_rows(sender_turned[:, j : j + 1], node_rows, rows)
                for j in range(i * blocks, (i + 1) * blocks)
            ],
            axis=0,
        )
        start = pre[span] if i < AHEAD else near_part(i)
        hidden = halved_silu(start + dot(marks, far))
        y = dot(hidden, w2c)
        scale = inverse_spread(y, ones)
        slot = lax.broadcasted_iota(jnp.int32, scale.shape, 0) + i * CHUNK
        scale = jnp.where(slot < live, scale, 0.0)
        scale = jnp.concatenate([scale] * (width // LANES), axis=1)
        update = (y * scale * gain[...]).astype(BF16)
        fresh[span] = edges[span] + update
        copy = pltpu.make_async_copy(fresh.at[span], new_edges.at[span], store_sem.at[i])
        copy.start()
        stores.append(copy)
        ids = row_ids(node_rows)
        member = jnp.concatenate(
            [
                mark(
                    jnp.broadcast_to(receivers[j : j + 1], (node_rows, LANES)).astype(jnp.int16)
                    == ids
                )
                for j in range(i * blocks, (i + 1) * blocks)
            ],
            axis=1,
        )
        messages = messages + dot(member, update)

    node_pre = node_pre + dot(messages.astype(BF16), v1[width:])
    z = dot(halved_silu(0.5 * node_pre), v2c)
    scale = inverse_spread(z, ones)
    scale = jnp.concatenate([scale] * (width // LANES), axis=1)
    fresh_nodes[...] = (own.astype(F32) + z * scale * ngain[...]).astype(BF16)
    copy = pltpu.make_async_copy(fresh_nodes, new_nodes, store_sem.at[chunks])
    copy.start()
    stores.append(copy)

    for copy in band:
        copy.wait_send()

    @pl.when(a < n_lat - 1)
    def _():
        rims[0].wait_send()

    @pl.when(a > 0)
    def _():
        rims[1].wait_send()

    for copy in stores:
        copy.wait()


def local(
    n_lat,
    n_lon,
    nodes,
    edges,
    senders,
    receivers,
    edge_count,
    send_index,
    rim_index,
    edge_w1,
    edge_b1,
    edge_w2,
    edge_gain,
    node_w1,
    node_b1,
    node_w2,
    node_gain,
):
    node_rows, width = nodes.shape
    edge_rows = edges.shape[0]
    halo, rim = send_index.shape[1], rim_index.shape[1]
    listed = n_lon * halo + 2 * rim
    chunks = edge_rows // CHUNK
    operands = (
        nodes,
        edge_w1,
        send_index,
        rim_index,
        senders.reshape(-1, LANES),
        receivers.reshape(-1, LANES),
        edge_b1.reshape(1, width),
        edge_gain.reshape(1, width),
        node_b1.reshape(1, width),
        node_gain.reshape(1, width),
        edge_w2,
        node_w1,
        node_w2,
        edges,
    )
    hbm = pl.BlockSpec(memory_space=pltpu.HBM)
    return pl.pallas_call(
        functools.partial(kernel, n_lat, n_lon),
        out_shape=(
            jax.ShapeDtypeStruct(nodes.shape, BF16),
            jax.ShapeDtypeStruct(edges.shape, BF16),
        ),
        in_specs=[pl.BlockSpec(memory_space=pltpu.SMEM)] + [hbm] * len(operands),
        out_specs=(hbm, hbm),
        scratch_shapes=[pltpu.VMEM(x.shape, x.dtype) for x in operands]
        + [
            pltpu.VMEM((node_rows + listed, width), BF16),
            pltpu.VMEM((listed, width), BF16),
            pltpu.VMEM((edge_rows, width), F32),
            pltpu.VMEM(edges.shape, BF16),
            pltpu.VMEM(nodes.shape, BF16),
            pltpu.SemaphoreType.DMA((len(operands),)),
            pltpu.SemaphoreType.DMA((chunks + 1,)),
            pltpu.SemaphoreType.DMA((n_lon + 1,)),
            pltpu.SemaphoreType.DMA((n_lon + 1,)),
        ],
        compiler_params=pltpu.CompilerParams(
            collective_id=0, has_side_effects=True, vmem_limit_bytes=60 * 1024 * 1024
        ),
    )(edge_count, *operands)


def solution(mesh):
    rows, flat = P(("lat", "lon"), None), P(("lat", "lon"))
    return jax.shard_map(
        functools.partial(local, mesh.shape["lat"], mesh.shape["lon"]),
        mesh=mesh,
        in_specs=(rows, rows, flat, flat, flat, rows, rows) + (P(),) * 8,
        out_specs=(rows, rows),
        check_vma=False,
    )
```

```python
import functools

import jax
import jax.numpy as jnp
from jax import lax
from jax.experimental import pallas as pl
from jax.experimental.pallas import tpu as pltpu
from jax.sharding import PartitionSpec as P

BF16 = jnp.bfloat16
F32 = jnp.float32
MESH = pl.DeviceIdType.MESH
LANES = 128
CHUNK = 512


def dot(a, b):
    return jnp.dot(a, b, preferred_element_type=F32)


def lane_ids(rows):
    return lax.broadcasted_iota(jnp.int32, (rows, LANES), 1).astype(jnp.int16)


def row_ids(rows):
    return lax.broadcasted_iota(jnp.int32, (rows, LANES), 0).astype(jnp.int16)


def mark(hit):
    return jnp.where(hit, jnp.ones(hit.shape, BF16), jnp.zeros(hit.shape, BF16))


def pick_rows(columns, low, high):
    n = columns.shape[0]
    spread = jnp.broadcast_to(columns, (n, LANES)).astype(jnp.int16)
    lanes = lane_ids(n)
    tiles = [mark(spread == lanes + jnp.int16(t)) for t in range(low, high, LANES)]
    return jnp.concatenate(tiles, axis=1)


def turned(block):
    short = LANES - block.shape[0]
    if short:
        block = jnp.concatenate([block, jnp.zeros((short, LANES), jnp.int32)], axis=0)
    return jnp.transpose(block)


def centred_weights(w):
    w = w.astype(F32)
    return (w - jnp.mean(w, axis=-1, keepdims=True)).astype(BF16)


def halved_silu(h):
    return (h + h * jnp.tanh(h)).astype(BF16)


def inverse_spread(y, ones):
    return lax.rsqrt(dot((y * y).astype(BF16), ones) + 1e-05)


def exchange(
    n_lat,
    n_lon,
    nodes_in,
    w1_in,
    send_index_in,
    rim_index_in,
    senders_in,
    b1_in,
    c1_in,
    w2_in,
    v2_in,
    receivers_in,
    gain_in,
    ngain_in,
    v1_in,
    edges_in,
    far,
    pre,
    node_pre,
    w2c,
    v2c,
    sender_turned,
    nodes,
    receivers,
    gain,
    ngain,
    v1,
    edges,
    w1,
    send_index,
    rim_index,
    senders,
    b1,
    c1,
    w2,
    v2,
    outgoing,
    load_sem,
    send_sem,
    recv_sem,
):
    a, b = lax.axis_index("lat"), lax.axis_index("lon")
    node_rows, width = nodes.shape
    halo = send_index.shape[1]
    rim = rim_index.shape[1]
    rim_at = n_lon * halo
    chunks = edges.shape[0] // CHUNK
    blocks = CHUNK // LANES

    barrier = pltpu.get_barrier_semaphore()
    for d in range(1, n_lon):
        pl.semaphore_signal(
            barrier, inc=1, device_id=(a, lax.rem(b + d, n_lon)), device_id_type=MESH
        )

    @pl.when(a > 0)
    def _():
        pl.semaphore_signal(barrier, inc=1, device_id=(a - 1, b), device_id_type=MESH)

    @pl.when(a < n_lat - 1)
    def _():
        pl.semaphore_signal(barrier, inc=1, device_id=(a + 1, b), device_id_type=MESH)

    pairs = [
        (nodes_in, nodes),
        (w1_in, w1),
        (send_index_in, send_index),
        (rim_index_in, rim_index),
        (senders_in, senders),
        (b1_in, b1),
        (c1_in, c1),
        (w2_in, w2),
        (v2_in, v2),
        (receivers_in, receivers),
        (gain_in, gain),
        (ngain_in, ngain),
        (v1_in, v1),
        (edges_in, edges),
    ]
    loads = [
        pltpu.make_async_copy(src, dst, load_sem.at[i]) for i, (src, dst) in enumerate(pairs)
    ]
    for copy in loads:
        copy.start()
    for copy in loads[:4]:
        copy.wait()

    lists = jnp.concatenate(
        [send_index[...], jnp.zeros((n_lon, LANES - halo), jnp.int32)], axis=1
    )
    list_turned = turned(jnp.concatenate([rim_index[...], lists], axis=0))
    own = nodes[...]
    by_sender = (0.5 * dot(own, w1[width : 2 * width])).astype(BF16)
    for p in range(n_lon):
        chosen = pick_rows(list_turned[:halo, 2 + p : 3 + p], 0, node_rows)
        outgoing[p * halo : (p + 1) * halo] = dot(chosen, by_sender).astype(BF16)
    for side in range(2):
        chosen = pick_rows(list_turned[:, side : side + 1], 0, node_rows)
        at = n_lon * halo + side * rim
        outgoing[at : at + rim] = dot(chosen, by_sender).astype(BF16)
    mine = pl.multiple_of(b * halo, halo)
    far[pl.ds(mine, halo)] = outgoing[pl.ds(mine, halo)]

    @pl.when(a == 0)
    def _():
        far[rim_at : rim_at + rim] = jnp.zeros((rim, width), BF16)

    @pl.when(a == n_lat - 1)
    def _():
        far[rim_at + rim :] = jnp.zeros((rim, width), BF16)

    below = jnp.where(a > 0, 1, 0)
    above = jnp.where(a < n_lat - 1, 1, 0)
    pl.semaphore_wait(barrier, n_lon - 1 + below + above)
    band = []
    for d in range(1, n_lon):
        p = lax.rem(b + d, n_lon)
        copy = pltpu.make_async_remote_copy(
            src_ref=outgoing.at[pl.ds(pl.multiple_of(p * halo, halo), halo)],
            dst_ref=far.at[pl.ds(mine, halo)],
            send_sem=send_sem.at[d - 1],
            recv_sem=recv_sem.at[d - 1],
            device_id=(a, p),
            device_id_type=MESH,
        )
        copy.start()
        band.append(copy)
    rims = [
        pltpu.make_async_remote_copy(
            src_ref=outgoing.at[pl.ds(n_lon * halo + side * rim, rim)],
            dst_ref=far.at[pl.ds(rim_at + side * rim, rim)],
            send_sem=send_sem.at[n_lon - 1 + side],
            recv_sem=recv_sem.at[n_lon - 1 + side],
            device_id=(a + 1 - 2 * side, b),
            device_id_type=MESH,
        )
        for side in range(2)
    ]

    @pl.when(a < n_lat - 1)
    def _():
        rims[0].start()

    @pl.when(a > 0)
    def _():
        rims[1].start()

    for copy in loads[4:]:
        copy.wait()
    sender_turned[...] = turned(senders[...])
    receiver_turned = turned(receivers[...])
    by_receiver = (0.5 * (dot(own, w1[2 * width :]) + b1[...])).astype(BF16)
    near = jnp.concatenate(
        [(0.5 * w1[:width].astype(F32)).astype(BF16), by_receiver, by_sender], axis=0
    )
    for i in range(chunks):
        span = slice(i * CHUNK, (i + 1) * CHUNK)
        marks = [
            jnp.concatenate(
                [
                    pick_rows(receiver_turned[:, j : j + 1], 0, node_rows),
                    pick_rows(sender_turned[:, j : j + 1], 0, node_rows),
                ],
                axis=1,
            )
            for j in range(i * blocks, (i + 1) * blocks)
        ]
        marks = jnp.concatenate(marks, axis=0)
        pre[span] = dot(jnp.concatenate([edges[span], marks], axis=1), near)
    w2c[...] = centred_weights(w2[...])
    v2c[...] = centred_weights(v2[...])
    node_pre[...] = 0.5 * (dot(own, v1[:width]) + c1[...])

    for copy in band:
        copy.wait()

    @pl.when(a < n_lat - 1)
    def _():
        rims[0].wait_send()
        rims[1].wait_recv()

    @pl.when(a > 0)
    def _():
        rims[1].wait_send()
        rims[0].wait_recv()


def finish(
    count,
    far,
    pre,
    node_pre,
    w2c,
    v2c,
    sender_turned,
    nodes,
    receivers,
    gain,
    ngain,
    v1,
    edges,
    new_nodes,
    new_edges,
    fresh,
    fresh_nodes,
    store_sem,
):
    node_rows, width = nodes.shape
    chunks = edges.shape[0] // CHUNK
    blocks = CHUNK // LANES
    ones = jnp.full((width, LANES), 1.0 / width, BF16)
    live = count[0]
    messages = jnp.zeros((node_rows, width), F32)
    ids = row_ids(node_rows)
    stores = []
    for i in range(chunks):
        span = slice(i * CHUNK, (i + 1) * CHUNK)
        marks = [
            pick_rows(sender_turned[:, j : j + 1], node_rows, node_rows + far.shape[0])
            for j in range(i * blocks, (i + 1) * blocks)
        ]
        hidden = halved_silu(pre[span] + dot(jnp.concatenate(marks, axis=0), far[...]))
        y = dot(hidden, w2c[...])
        scale = inverse_spread(y, ones)
        slot = lax.broadcasted_iota(jnp.int32, scale.shape, 0) + i * CHUNK
        scale = jnp.where(slot < live, scale, 0.0)
        scale = jnp.concatenate([scale] * (width // LANES), axis=1)
        update = (y * scale * gain[...]).astype(BF16)
        fresh[span] = edges[span] + update
        copy = pltpu.make_async_copy(fresh.at[span], new_edges.at[span], store_sem.at[i])
        copy.start()
        stores.append(copy)
        member = [
            mark(jnp.broadcast_to(receivers[j : j + 1], ids.shape).astype(jnp.int16) == ids)
            for j in range(i * blocks, (i + 1) * blocks)
        ]
        messages = messages + dot(jnp.concatenate(member, axis=1), update)

    h = node_pre[...] + 0.5 * dot(messages.astype(BF16), v1[width:])
    z = dot(halved_silu(h), v2c[...])
    scale = inverse_spread(z, ones)
    scale = jnp.concatenate([scale] * (width // LANES), axis=1)
    fresh_nodes[...] = (nodes[...].astype(F32) + z * scale * ngain[...]).astype(BF16)
    copy = pltpu.make_async_copy(fresh_nodes, new_nodes, store_sem.at[chunks])
    copy.start()
    for copy in stores + [copy]:
        copy.wait()


def in_hbm(x):
    return pltpu.with_memory_space_constraint(x, pltpu.HBM)


def local(
    n_lat,
    n_lon,
    nodes,
    edges,
    senders,
    receivers,
    edge_count,
    send_index,
    rim_index,
    edge_w1,
    edge_b1,
    edge_w2,
    edge_gain,
    node_w1,
    node_b1,
    node_w2,
    node_gain,
):
    width = nodes.shape[1]
    listed = n_lon * send_index.shape[1] + 2 * rim_index.shape[1]
    inner = (
        nodes,
        edge_w1,
        send_index,
        rim_index,
        senders.reshape(-1, LANES),
        edge_b1.reshape(1, width),
        node_b1.reshape(1, width),
        edge_w2,
        node_w2,
    )
    passed = (
        receivers.reshape(-1, LANES),
        edge_gain.reshape(1, width),
        node_gain.reshape(1, width),
        node_w1,
        edges,
    )
    operands = [in_hbm(x) for x in inner + passed]
    handed = [
        ((listed, width), BF16),
        (edges.shape, F32),
        (nodes.shape, F32),
        (edge_w2.shape, BF16),
        (node_w2.shape, BF16),
        ((LANES, LANES), jnp.int32),
        (nodes.shape, BF16),
    ] + [(x.shape, x.dtype) for x in passed]
    hbm = pl.BlockSpec(memory_space=pltpu.HBM)
    vmem = pl.BlockSpec(memory_space=pltpu.VMEM)
    limit = 24 * 1024 * 1024
    between = pl.pallas_call(
        functools.partial(exchange, n_lat, n_lon),
        out_shape=tuple(pltpu.VMEM(shape, dtype) for shape, dtype in handed),
        in_specs=[hbm] * len(operands),
        out_specs=(vmem,) * len(handed),
        scratch_shapes=[pltpu.VMEM(x.shape, x.dtype) for x in inner[1:]]
        + [
            pltpu.VMEM((listed, width), BF16),
            pltpu.SemaphoreType.DMA((len(operands),)),
            pltpu.SemaphoreType.DMA((n_lon + 1,)),
            pltpu.SemaphoreType.DMA((n_lon + 1,)),
        ],
        compiler_params=pltpu.CompilerParams(
            collective_id=0, has_side_effects=True, vmem_limit_bytes=limit
        ),
    )(*operands)
    chunks = edges.shape[0] // CHUNK
    return pl.pallas_call(
        finish,
        out_shape=(pltpu.HBM(nodes.shape, BF16), pltpu.HBM(edges.shape, BF16)),
        in_specs=[pl.BlockSpec(memory_space=pltpu.SMEM)] + [vmem] * len(handed),
        out_specs=(hbm, hbm),
        scratch_shapes=[
            pltpu.VMEM(edges.shape, BF16),
            pltpu.VMEM(nodes.shape, BF16),
            pltpu.SemaphoreType.DMA((chunks + 1,)),
        ],
        compiler_params=pltpu.CompilerParams(vmem_limit_bytes=limit),
    )(edge_count, *between)


def solution(mesh):
    rows, flat = P(("lat", "lon"), None), P(("lat", "lon"))
    return jax.shard_map(
        functools.partial(local, mesh.shape["lat"], mesh.shape["lon"]),
        mesh=mesh,
        in_specs=(rows, rows, flat, flat, flat, rows, rows) + (P(),) * 8,
        out_specs=(rows, rows),
        check_vma=False,
    )
```

```python
import functools

import jax
import jax.numpy as jnp
from jax import lax
from jax.experimental import pallas as pl
from jax.experimental.pallas import tpu as pltpu
from jax.sharding import PartitionSpec as P

BF16 = jnp.bfloat16
F32 = jnp.float32
MESH = pl.DeviceIdType.MESH
LANES = 128
CHUNK = 512
AHEAD = 4


def dot(a, b):
    return jnp.dot(a, b, preferred_element_type=F32)


def lane_ids(rows):
    return lax.broadcasted_iota(jnp.int32, (rows, LANES), 1).astype(jnp.int16)


def row_ids(rows):
    return lax.broadcasted_iota(jnp.int32, (rows, LANES), 0).astype(jnp.int16)


def mark(hit):
    return jnp.where(hit, jnp.ones(hit.shape, BF16), jnp.zeros(hit.shape, BF16))


def pick_rows(columns, low, high):
    n = columns.shape[0]
    spread = jnp.broadcast_to(columns, (n, LANES)).astype(jnp.int16)
    lanes = lane_ids(n)
    tiles = [mark(spread == lanes + jnp.int16(t)) for t in range(low, high, LANES)]
    return jnp.concatenate(tiles, axis=1)


def turned(block):
    short = LANES - block.shape[0]
    if short:
        block = jnp.concatenate([block, jnp.zeros((short, LANES), jnp.int32)], axis=0)
    return jnp.transpose(block)


def centred_weights(w):
    w = w.astype(F32)
    return (w - jnp.mean(w, axis=-1, keepdims=True)).astype(BF16)


def halved_silu(h):
    return (h + h * jnp.tanh(h)).astype(BF16)


def inverse_spread(y, ones):
    return lax.rsqrt(dot((y * y).astype(BF16), ones) + 1e-05)


def exchange(
    n_lat,
    n_lon,
    rim_index_in,
    nodes_in,
    w1_in,
    send_index_in,
    senders_in,
    b1_in,
    c1_in,
    w2_in,
    v2_in,
    receivers_in,
    gain_in,
    ngain_in,
    v1_in,
    edges_in,
    rims_far,
    marks_far,
    member,
    pre,
    node_pre,
    w2c,
    v2c,
    nodes,
    gain,
    ngain,
    v1,
    edges,
    rim_index,
    w1,
    send_index,
    senders,
    b1,
    c1,
    w2,
    v2,
    receivers,
    band_far,
    outgoing,
    load_sem,
    send_sem,
    recv_sem,
):
    a, b = lax.axis_index("lat"), lax.axis_index("lon")
    node_rows, width = nodes.shape
    halo = send_index.shape[1]
    rim = rim_index.shape[1]
    rim_from = node_rows + n_lon * halo
    rim_to = rim_from + 2 * rim
    chunks = edges.shape[0] // CHUNK
    blocks = CHUNK // LANES

    barrier = pltpu.get_barrier_semaphore()
    for d in range(1, n_lon):
        pl.semaphore_signal(
            barrier, inc=1, device_id=(a, lax.rem(b + d, n_lon)), device_id_type=MESH
        )

    @pl.when(a > 0)
    def _():
        pl.semaphore_signal(barrier, inc=1, device_id=(a - 1, b), device_id_type=MESH)

    @pl.when(a < n_lat - 1)
    def _():
        pl.semaphore_signal(barrier, inc=1, device_id=(a + 1, b), device_id_type=MESH)

    sender_rows = pl.ds(width, width)
    pairs = [
        (rim_index_in, rim_index),
        (nodes_in, nodes),
        (w1_in.at[sender_rows], w1.at[sender_rows]),
        (send_index_in, send_index),
        (senders_in, senders),
        (receivers_in, receivers),
        (w1_in.at[pl.ds(0, width)], w1.at[pl.ds(0, width)]),
        (w1_in.at[pl.ds(2 * width, width)], w1.at[pl.ds(2 * width, width)]),
        (b1_in, b1),
        (edges_in, edges),
        (c1_in, c1),
        (w2_in, w2),
        (v2_in, v2),
        (gain_in, gain),
        (ngain_in, ngain),
        (v1_in, v1),
    ]
    loads = [
        pltpu.make_async_copy(src, dst, load_sem.at[i]) for i, (src, dst) in enumerate(pairs)
    ]
    for copy in loads:
        copy.start()

    @pl.when(a == 0)
    def _():
        rims_far[:rim] = jnp.zeros((rim, width), BF16)

    @pl.when(a == n_lat - 1)
    def _():
        rims_far[rim:] = jnp.zeros((rim, width), BF16)

    for copy in loads[:4]:
        copy.wait()
    lists = jnp.concatenate(
        [send_index[...], jnp.zeros((n_lon, LANES - halo), jnp.int32)], axis=1
    )
    list_turned = turned(jnp.concatenate([rim_index[...], lists], axis=0))
    own = nodes[...]
    by_sender = (0.5 * dot(own, w1[sender_rows])).astype(BF16)
    chosen = [pick_rows(list_turned[:, side : side + 1], 0, node_rows) for side in range(2)]
    outgoing[: 2 * rim] = dot(jnp.concatenate(chosen, axis=0), by_sender).astype(BF16)

    below = jnp.where(a > 0, 1, 0)
    above = jnp.where(a < n_lat - 1, 1, 0)
    pl.semaphore_wait(barrier, n_lon - 1 + below + above)
    rims = [
        pltpu.make_async_remote_copy(
            src_ref=outgoing.at[pl.ds(side * rim, rim)],
            dst_ref=rims_far.at[pl.ds(side * rim, rim)],
            send_sem=send_sem.at[n_lon - 1 + side],
            recv_sem=recv_sem.at[n_lon - 1 + side],
            device_id=(a + 1 - 2 * side, b),
            device_id_type=MESH,
        )
        for side in range(2)
    ]

    @pl.when(a < n_lat - 1)
    def _():
        rims[0].start()

    @pl.when(a > 0)
    def _():
        rims[1].start()

    chosen = [
        pick_rows(list_turned[:halo, 2 + p : 3 + p], 0, node_rows) for p in range(n_lon)
    ]
    outgoing[2 * rim :] = dot(jnp.concatenate(chosen, axis=0), by_sender).astype(BF16)
    mine = pl.multiple_of(b * halo, halo)
    band = []
    for d in range(1, n_lon):
        p = lax.rem(b + d, n_lon)
        copy = pltpu.make_async_remote_copy(
            src_ref=outgoing.at[pl.ds(2 * rim + pl.multiple_of(p * halo, halo), halo)],
            dst_ref=band_far.at[pl.ds(mine, halo)],
            send_sem=send_sem.at[d - 1],
            recv_sem=recv_sem.at[d - 1],
            device_id=(a, p),
            device_id_type=MESH,
        )
        copy.start()
        band.append(copy)
    band_far[pl.ds(mine, halo)] = outgoing[pl.ds(2 * rim + mine, halo)]

    for copy in loads[4:]:
        copy.wait()
    sender_turned = turned(senders[...])
    receiver_turned = turned(receivers[...])
    by_receiver = (0.5 * (dot(own, w1[2 * width :]) + b1[...])).astype(BF16)
    near = jnp.concatenate(
        [(0.5 * w1[:width].astype(F32)).astype(BF16), by_receiver, by_sender], axis=0
    )

    def marks(turned_rows, i, low, high):
        rows = [
            pick_rows(turned_rows[:, j : j + 1], low, high)
            for j in range(i * blocks, (i + 1) * blocks)
        ]
        return jnp.concatenate(rows, axis=0)

    def near_part(i):
        span = slice(i * CHUNK, (i + 1) * CHUNK)
        marks_far[span] = marks(sender_turned, i, rim_from, rim_to)
        row = [
            mark(jnp.broadcast_to(receivers[j : j + 1], ids.shape).astype(jnp.int16) == ids)
            for j in range(i * blocks, (i + 1) * blocks)
        ]
        member[:, span] = jnp.concatenate(row, axis=1)
        rows = [
            edges[span],
            marks(receiver_turned, i, 0, node_rows),
            marks(sender_turned, i, 0, node_rows),
        ]
        return rows

    ids = row_ids(node_rows)
    ahead = min(AHEAD, chunks)
    for i in range(ahead):
        pre[i * CHUNK : (i + 1) * CHUNK] = dot(jnp.concatenate(near_part(i), axis=1), near)
    w2c[...] = centred_weights(w2[...])
    v2c[...] = centred_weights(v2[...])
    node_pre[...] = 0.5 * (dot(own, v1[:width]) + c1[...])

    for copy in band:
        copy.wait()
    from_band = band_far[...]
    for i in range(ahead):
        pre[i * CHUNK : (i + 1) * CHUNK] += dot(
            marks(sender_turned, i, node_rows, rim_from), from_band
        )
    wide = jnp.concatenate([near, from_band], axis=0)
    for i in range(ahead, chunks):
        rows = near_part(i) + [marks(sender_turned, i, node_rows, rim_from)]
        pre[i * CHUNK : (i + 1) * CHUNK] = dot(jnp.concatenate(rows, axis=1), wide)

    @pl.when(a < n_lat - 1)
    def _():
        rims[0].wait_send()
        rims[1].wait_recv()

    @pl.when(a > 0)
    def _():
        rims[1].wait_send()
        rims[0].wait_recv()


def finish(
    count,
    rims_far,
    marks_far,
    member,
    pre,
    node_pre,
    w2c,
    v2c,
    nodes,
    gain,
    ngain,
    v1,
    edges,
    new_nodes,
    new_edges,
    fresh,
    fresh_nodes,
    store_sem,
):
    node_rows, width = nodes.shape
    chunks = edges.shape[0] // CHUNK
    ones = jnp.full((width, LANES), 1.0 / width, BF16)
    live = count[0]
    messages = jnp.zeros((node_rows, width), F32)
    stores = []
    for i in range(chunks):
        span = slice(i * CHUNK, (i + 1) * CHUNK)
        hidden = halved_silu(pre[span] + dot(marks_far[span], rims_far[...]))
        y = dot(hidden, w2c[...])
        scale = inverse_spread(y, ones)
        slot = lax.broadcasted_iota(jnp.int32, scale.shape, 0) + i * CHUNK
        scale = jnp.where(slot < live, scale, 0.0)
        scale = jnp.concatenate([scale] * (width // LANES), axis=1)
        update = (y * scale * gain[...]).astype(BF16)
        fresh[span] = edges[span] + update
        copy = pltpu.make_async_copy(fresh.at[span], new_edges.at[span], store_sem.at[i])
        copy.start()
        stores.append(copy)
        messages = messages + dot(member[:, span], update)

    h = node_pre[...] + 0.5 * dot(messages.astype(BF16), v1[width:])
    z = dot(halved_silu(h), v2c[...])
    scale = inverse_spread(z, ones)
    scale = jnp.concatenate([scale] * (width // LANES), axis=1)
    fresh_nodes[...] = (nodes[...].astype(F32) + z * scale * ngain[...]).astype(BF16)
    copy = pltpu.make_async_copy(fresh_nodes, new_nodes, store_sem.at[chunks])
    copy.start()
    for copy in stores + [copy]:
        copy.wait()


def in_hbm(x):
    return pltpu.with_memory_space_constraint(x, pltpu.HBM)


def local(
    n_lat,
    n_lon,
    nodes,
    edges,
    senders,
    receivers,
    edge_count,
    send_index,
    rim_index,
    edge_w1,
    edge_b1,
    edge_w2,
    edge_gain,
    node_w1,
    node_b1,
    node_w2,
    node_gain,
):
    width = nodes.shape[1]
    inner = (
        rim_index,
        nodes,
        edge_w1,
        send_index,
        senders.reshape(-1, LANES),
        edge_b1.reshape(1, width),
        node_b1.reshape(1, width),
        edge_w2,
        node_w2,
        receivers.reshape(-1, LANES),
    )
    passed = (
        edge_gain.reshape(1, width),
        node_gain.reshape(1, width),
        node_w1,
        edges,
    )
    operands = [in_hbm(x) for x in inner + passed]
    node_rows, edge_rows = nodes.shape[0], edges.shape[0]
    band_rows, rim_rows = n_lon * send_index.shape[1], 2 * rim_index.shape[1]
    handed = [
        ((rim_rows, width), BF16),
        ((edge_rows, rim_rows), BF16),
        ((node_rows, edge_rows), BF16),
        (edges.shape, F32),
        (nodes.shape, F32),
        (edge_w2.shape, BF16),
        (node_w2.shape, BF16),
        (nodes.shape, BF16),
    ] + [(x.shape, x.dtype) for x in passed]
    scratch = [x for x in inner if x is not nodes]
    hbm = pl.BlockSpec(memory_space=pltpu.HBM)
    vmem = pl.BlockSpec(memory_space=pltpu.VMEM)
    limit = 24 * 1024 * 1024
    between = pl.pallas_call(
        functools.partial(exchange, n_lat, n_lon),
        out_shape=tuple(pltpu.VMEM(shape, dtype) for shape, dtype in handed),
        in_specs=[hbm] * len(operands),
        out_specs=(vmem,) * len(handed),
        scratch_shapes=[pltpu.VMEM(x.shape, x.dtype) for x in scratch]
        + [
            pltpu.VMEM((band_rows, width), BF16),
            pltpu.VMEM((rim_rows + band_rows, width), BF16),
            pltpu.SemaphoreType.DMA((len(operands) + 2,)),
            pltpu.SemaphoreType.DMA((n_lon + 1,)),
            pltpu.SemaphoreType.DMA((n_lon + 1,)),
        ],
        compiler_params=pltpu.CompilerParams(
            collective_id=0, has_side_effects=True, vmem_limit_bytes=limit
        ),
    )(*operands)
    chunks = edges.shape[0] // CHUNK
    return pl.pallas_call(
        finish,
        out_shape=(pltpu.HBM(nodes.shape, BF16), pltpu.HBM(edges.shape, BF16)),
        in_specs=[pl.BlockSpec(memory_space=pltpu.SMEM)] + [vmem] * len(handed),
        out_specs=(hbm, hbm),
        scratch_shapes=[
            pltpu.VMEM(edges.shape, BF16),
            pltpu.VMEM(nodes.shape, BF16),
            pltpu.SemaphoreType.DMA((chunks + 1,)),
        ],
        compiler_params=pltpu.CompilerParams(vmem_limit_bytes=limit),
    )(edge_count, *between)


def solution(mesh):
    rows, flat = P(("lat", "lon"), None), P(("lat", "lon"))
    return jax.shard_map(
        functools.partial(local, mesh.shape["lat"], mesh.shape["lon"]),
        mesh=mesh,
        in_specs=(rows, rows, flat, flat, flat, rows, rows) + (P(),) * 8,
        out_specs=(rows, rows),
        check_vma=False,
    )
```

```python
import functools

import jax
import jax.numpy as jnp
from jax import lax
from jax.experimental import pallas as pl
from jax.experimental.pallas import tpu as pltpu
from jax.sharding import PartitionSpec as P

BF16 = jnp.bfloat16
F32 = jnp.float32
MESH = pl.DeviceIdType.MESH
LANES = 128
CHUNK = 512
STEP = 256
AHEAD = 4


def dot(a, b):
    return jnp.dot(a, b, preferred_element_type=F32)


def lane_ids(rows):
    return lax.broadcasted_iota(jnp.int32, (rows, LANES), 1).astype(jnp.int16)


def row_ids(rows):
    return lax.broadcasted_iota(jnp.int32, (rows, LANES), 0).astype(jnp.int16)


def mark(hit):
    return jnp.where(hit, jnp.ones(hit.shape, BF16), jnp.zeros(hit.shape, BF16))


def pick_rows(columns, low, high):
    n = columns.shape[0]
    spread = jnp.broadcast_to(columns, (n, LANES)).astype(jnp.int16)
    lanes = lane_ids(n)
    tiles = [mark(spread == lanes + jnp.int16(t)) for t in range(low, high, LANES)]
    return jnp.concatenate(tiles, axis=1)


def turned(block):
    short = LANES - block.shape[0]
    if short:
        block = jnp.concatenate([block, jnp.zeros((short, LANES), jnp.int32)], axis=0)
    return jnp.transpose(block)


def centred_weights(w):
    w = w.astype(F32)
    return (w - jnp.mean(w, axis=-1, keepdims=True)).astype(BF16)


def halved_silu(h):
    return (h + h * jnp.tanh(h)).astype(BF16)


def inverse_spread(y, ones):
    return lax.rsqrt(dot((y * y).astype(BF16), ones) + 1e-05)


def exchange(
    n_lat,
    n_lon,
    rim_index_in,
    nodes_in,
    w1_in,
    send_index_in,
    senders_in,
    b1_in,
    c1_in,
    w2_in,
    v2_in,
    receivers_in,
    gain_in,
    ngain_in,
    v1_in,
    edges_in,
    rims_far,
    marks_far,
    member,
    pre,
    node_pre,
    w2c,
    v2c,
    nodes,
    gain,
    ngain,
    v1,
    edges,
    rim_index,
    w1,
    send_index,
    senders,
    b1,
    c1,
    w2,
    v2,
    receivers,
    band_far,
    outgoing,
    load_sem,
    send_sem,
    recv_sem,
):
    a, b = lax.axis_index("lat"), lax.axis_index("lon")
    node_rows, width = nodes.shape
    halo = send_index.shape[1]
    rim = rim_index.shape[1]
    rim_from = node_rows + n_lon * halo
    rim_to = rim_from + 2 * rim
    chunks = edges.shape[0] // CHUNK
    blocks = CHUNK // LANES

    barrier = pltpu.get_barrier_semaphore()
    for d in range(1, n_lon):
        pl.semaphore_signal(
            barrier, inc=1, device_id=(a, lax.rem(b + d, n_lon)), device_id_type=MESH
        )

    @pl.when(a > 0)
    def _():
        pl.semaphore_signal(barrier, inc=1, device_id=(a - 1, b), device_id_type=MESH)

    @pl.when(a < n_lat - 1)
    def _():
        pl.semaphore_signal(barrier, inc=1, device_id=(a + 1, b), device_id_type=MESH)

    sender_rows = pl.ds(width, width)
    pairs = [
        (rim_index_in, rim_index),
        (nodes_in, nodes),
        (w1_in.at[sender_rows], w1.at[sender_rows]),
        (send_index_in, send_index),
        (senders_in, senders),
        (receivers_in, receivers),
        (w1_in.at[pl.ds(0, width)], w1.at[pl.ds(0, width)]),
        (w1_in.at[pl.ds(2 * width, width)], w1.at[pl.ds(2 * width, width)]),
        (b1_in, b1),
        (edges_in, edges),
        (c1_in, c1),
        (w2_in, w2),
        (v2_in, v2),
        (gain_in, gain),
        (ngain_in, ngain),
        (v1_in, v1),
    ]
    loads = [
        pltpu.make_async_copy(src, dst, load_sem.at[i]) for i, (src, dst) in enumerate(pairs)
    ]
    for copy in loads:
        copy.start()

    @pl.when(a == 0)
    def _():
        rims_far[:rim] = jnp.zeros((rim, width), BF16)

    @pl.when(a == n_lat - 1)
    def _():
        rims_far[rim:] = jnp.zeros((rim, width), BF16)

    for copy in loads[:4]:
        copy.wait()
    lists = jnp.concatenate(
        [send_index[...], jnp.zeros((n_lon, LANES - halo), jnp.int32)], axis=1
    )
    list_turned = turned(jnp.concatenate([rim_index[...], lists], axis=0))
    own = nodes[...]
    by_sender = (0.5 * dot(own, w1[sender_rows])).astype(BF16)
    chosen = [pick_rows(list_turned[:, side : side + 1], 0, node_rows) for side in range(2)]
    outgoing[: 2 * rim] = dot(jnp.concatenate(chosen, axis=0), by_sender).astype(BF16)

    chosen = [
        pick_rows(list_turned[:halo, 2 + p : 3 + p], 0, node_rows) for p in range(n_lon)
    ]
    outgoing[2 * rim :] = dot(jnp.concatenate(chosen, axis=0), by_sender).astype(BF16)
    for copy in loads[4:]:
        copy.wait()
    sender_turned = turned(senders[...])
    receiver_turned = turned(receivers[...])
    by_receiver = (0.5 * (dot(own, w1[2 * width :]) + b1[...])).astype(BF16)
    near = jnp.concatenate(
        [(0.5 * w1[:width].astype(F32)).astype(BF16), by_receiver, by_sender], axis=0
    )
    w2c[...] = centred_weights(w2[...])
    v2c[...] = centred_weights(v2[...])
    node_pre[...] = 0.5 * (dot(own, v1[:width]) + c1[...])

    below = jnp.where(a > 0, 1, 0)
    above = jnp.where(a < n_lat - 1, 1, 0)
    pl.semaphore_wait(barrier, n_lon - 1 + below + above)
    rims = [
        pltpu.make_async_remote_copy(
            src_ref=outgoing.at[pl.ds(side * rim, rim)],
            dst_ref=rims_far.at[pl.ds(side * rim, rim)],
            send_sem=send_sem.at[n_lon - 1 + side],
            recv_sem=recv_sem.at[n_lon - 1 + side],
            device_id=(a + 1 - 2 * side, b),
            device_id_type=MESH,
        )
        for side in range(2)
    ]

    @pl.when(a < n_lat - 1)
    def _():
        rims[0].start()

    @pl.when(a > 0)
    def _():
        rims[1].start()

    mine = pl.multiple_of(b * halo, halo)
    band = []
    for d in range(1, n_lon):
        p = lax.rem(b + d, n_lon)
        copy = pltpu.make_async_remote_copy(
            src_ref=outgoing.at[pl.ds(2 * rim + pl.multiple_of(p * halo, halo), halo)],
            dst_ref=band_far.at[pl.ds(mine, halo)],
            send_sem=send_sem.at[d - 1],
            recv_sem=recv_sem.at[d - 1],
            device_id=(a, p),
            device_id_type=MESH,
        )
        copy.start()
        band.append(copy)
    band_far[pl.ds(mine, halo)] = outgoing[pl.ds(2 * rim + mine, halo)]

    def marks(turned_rows, i, low, high):
        rows = [
            pick_rows(turned_rows[:, j : j + 1], low, high)
            for j in range(i * blocks, (i + 1) * blocks)
        ]
        return jnp.concatenate(rows, axis=0)

    def near_part(i):
        span = slice(i * CHUNK, (i + 1) * CHUNK)
        marks_far[span] = marks(sender_turned, i, rim_from, rim_to)
        row = [
            mark(jnp.broadcast_to(receivers[j : j + 1], ids.shape).astype(jnp.int16) == ids)
            for j in range(i * blocks, (i + 1) * blocks)
        ]
        member[:, span] = jnp.concatenate(row, axis=1)
        rows = [
            edges[span],
            marks(receiver_turned, i, 0, node_rows),
            marks(sender_turned, i, 0, node_rows),
        ]
        return rows

    ids = row_ids(node_rows)
    ahead = min(AHEAD, chunks)
    for i in range(ahead):
        pre[i * CHUNK : (i + 1) * CHUNK] = dot(jnp.concatenate(near_part(i), axis=1), near)
    for copy in band:
        copy.wait()
    from_band = band_far[...]
    for i in range(ahead):
        pre[i * CHUNK : (i + 1) * CHUNK] += dot(
            marks(sender_turned, i, node_rows, rim_from), from_band
        )
    wide = jnp.concatenate([near, from_band], axis=0)
    for i in range(ahead, chunks):
        rows = near_part(i) + [marks(sender_turned, i, node_rows, rim_from)]
        pre[i * CHUNK : (i + 1) * CHUNK] = dot(jnp.concatenate(rows, axis=1), wide)

    @pl.when(a < n_lat - 1)
    def _():
        rims[0].wait_send()
        rims[1].wait_recv()

    @pl.when(a > 0)
    def _():
        rims[1].wait_send()
        rims[0].wait_recv()


def finish(
    count,
    rims_far,
    marks_far,
    member,
    pre,
    node_pre,
    w2c,
    v2c,
    nodes,
    gain,
    ngain,
    v1,
    edges,
    new_nodes,
    new_edges,
    fresh,
    fresh_nodes,
    store_sem,
):
    node_rows, width = nodes.shape
    chunks = edges.shape[0] // STEP
    ones = jnp.full((width, LANES), 1.0 / width, BF16)
    live = count[0]
    messages = jnp.zeros((node_rows, width), F32)
    stores = []
    for i in range(chunks):
        span = slice(i * STEP, (i + 1) * STEP)
        hidden = halved_silu(pre[span] + dot(marks_far[span], rims_far[...]))
        y = dot(hidden, w2c[...])
        scale = inverse_spread(y, ones)
        slot = lax.broadcasted_iota(jnp.int32, scale.shape, 0) + i * STEP
        scale = jnp.where(slot < live, scale, 0.0)
        scale = jnp.concatenate([scale] * (width // LANES), axis=1)
        update = (y * scale * gain[...]).astype(BF16)
        fresh[span] = edges[span] + update
        copy = pltpu.make_async_copy(fresh.at[span], new_edges.at[span], store_sem.at[i])
        copy.start()
        stores.append(copy)
        messages = messages + dot(member[:, span], update)

    h = node_pre[...] + 0.5 * dot(messages.astype(BF16), v1[width:])
    z = dot(halved_silu(h), v2c[...])
    scale = inverse_spread(z, ones)
    scale = jnp.concatenate([scale] * (width // LANES), axis=1)
    fresh_nodes[...] = (nodes[...].astype(F32) + z * scale * ngain[...]).astype(BF16)
    copy = pltpu.make_async_copy(fresh_nodes, new_nodes, store_sem.at[chunks])
    copy.start()
    for copy in stores + [copy]:
        copy.wait()


def in_hbm(x):
    return pltpu.with_memory_space_constraint(x, pltpu.HBM)


def local(
    n_lat,
    n_lon,
    nodes,
    edges,
    senders,
    receivers,
    edge_count,
    send_index,
    rim_index,
    edge_w1,
    edge_b1,
    edge_w2,
    edge_gain,
    node_w1,
    node_b1,
    node_w2,
    node_gain,
):
    width = nodes.shape[1]
    inner = (
        rim_index,
        nodes,
        edge_w1,
        send_index,
        senders.reshape(-1, LANES),
        edge_b1.reshape(1, width),
        node_b1.reshape(1, width),
        edge_w2,
        node_w2,
        receivers.reshape(-1, LANES),
    )
    passed = (
        edge_gain.reshape(1, width),
        node_gain.reshape(1, width),
        node_w1,
        edges,
    )
    operands = [in_hbm(x) for x in inner + passed]
    node_rows, edge_rows = nodes.shape[0], edges.shape[0]
    band_rows, rim_rows = n_lon * send_index.shape[1], 2 * rim_index.shape[1]
    handed = [
        ((rim_rows, width), BF16),
        ((edge_rows, rim_rows), BF16),
        ((node_rows, edge_rows), BF16),
        (edges.shape, F32),
        (nodes.shape, F32),
        (edge_w2.shape, BF16),
        (node_w2.shape, BF16),
        (nodes.shape, BF16),
    ] + [(x.shape, x.dtype) for x in passed]
    scratch = [x for x in inner if x is not nodes]
    hbm = pl.BlockSpec(memory_space=pltpu.HBM)
    vmem = pl.BlockSpec(memory_space=pltpu.VMEM)
    limit = 24 * 1024 * 1024
    between = pl.pallas_call(
        functools.partial(exchange, n_lat, n_lon),
        out_shape=tuple(pltpu.VMEM(shape, dtype) for shape, dtype in handed),
        in_specs=[hbm] * len(operands),
        out_specs=(vmem,) * len(handed),
        scratch_shapes=[pltpu.VMEM(x.shape, x.dtype) for x in scratch]
        + [
            pltpu.VMEM((band_rows, width), BF16),
            pltpu.VMEM((rim_rows + band_rows, width), BF16),
            pltpu.SemaphoreType.DMA((len(operands) + 2,)),
            pltpu.SemaphoreType.DMA((n_lon + 1,)),
            pltpu.SemaphoreType.DMA((n_lon + 1,)),
        ],
        compiler_params=pltpu.CompilerParams(
            collective_id=0, has_side_effects=True, vmem_limit_bytes=limit
        ),
    )(*operands)
    chunks = edges.shape[0] // STEP
    return pl.pallas_call(
        finish,
        out_shape=(pltpu.HBM(nodes.shape, BF16), pltpu.HBM(edges.shape, BF16)),
        in_specs=[pl.BlockSpec(memory_space=pltpu.SMEM)] + [vmem] * len(handed),
        out_specs=(hbm, hbm),
        scratch_shapes=[
            pltpu.VMEM(edges.shape, BF16),
            pltpu.VMEM(nodes.shape, BF16),
            pltpu.SemaphoreType.DMA((chunks + 1,)),
        ],
        compiler_params=pltpu.CompilerParams(vmem_limit_bytes=limit),
    )(edge_count, *between)


def solution(mesh):
    rows, flat = P(("lat", "lon"), None), P(("lat", "lon"))
    return jax.shard_map(
        functools.partial(local, mesh.shape["lat"], mesh.shape["lon"]),
        mesh=mesh,
        in_specs=(rows, rows, flat, flat, flat, rows, rows) + (P(),) * 8,
        out_specs=(rows, rows),
        check_vma=False,
    )
```

```python
import functools

import jax
import jax.numpy as jnp
from jax import lax
from jax.experimental import pallas as pl
from jax.experimental.pallas import tpu as pltpu
from jax.sharding import PartitionSpec as P

BF16 = jnp.bfloat16
F32 = jnp.float32
MESH = pl.DeviceIdType.MESH
LANES = 128
CHUNK = 1024
AHEAD = 2


def dot(a, b):
    return jnp.dot(a, b, preferred_element_type=F32)


def lane_ids(rows):
    return lax.broadcasted_iota(jnp.int32, (rows, LANES), 1).astype(jnp.int16)


def row_ids(rows):
    return lax.broadcasted_iota(jnp.int32, (rows, LANES), 0).astype(jnp.int16)


def mark(hit):
    return jnp.where(hit, jnp.ones(hit.shape, BF16), jnp.zeros(hit.shape, BF16))


def pick_rows(columns, low, high):
    n = columns.shape[0]
    spread = jnp.broadcast_to(columns, (n, LANES)).astype(jnp.int16)
    lanes = lane_ids(n)
    tiles = [mark(spread == lanes + jnp.int16(t)) for t in range(low, high, LANES)]
    return jnp.concatenate(tiles, axis=1)


def turned(block):
    short = LANES - block.shape[0]
    if short:
        block = jnp.concatenate([block, jnp.zeros((short, LANES), jnp.int32)], axis=0)
    return jnp.transpose(block)


def centred_weights(w):
    w = w.astype(F32)
    return (w - jnp.mean(w, axis=-1, keepdims=True)).astype(BF16)


def halved_silu(h):
    return (h + h * jnp.tanh(h)).astype(BF16)


def inverse_spread(y, ones):
    return lax.rsqrt(dot((y * y).astype(BF16), ones) + 1e-05)


def exchange(
    n_lat,
    n_lon,
    rim_index_in,
    nodes_in,
    w1_in,
    send_index_in,
    senders_in,
    b1_in,
    c1_in,
    w2_in,
    v2_in,
    receivers_in,
    gain_in,
    ngain_in,
    v1_in,
    edges_in,
    rims_far,
    marks_far,
    member,
    pre,
    node_pre,
    w2c,
    v2c,
    nodes,
    gain,
    ngain,
    v1,
    edges,
    rim_index,
    w1,
    send_index,
    senders,
    b1,
    c1,
    w2,
    v2,
    receivers,
    band_far,
    outgoing,
    load_sem,
    send_sem,
    recv_sem,
):
    a, b = lax.axis_index("lat"), lax.axis_index("lon")
    node_rows, width = nodes.shape
    halo = send_index.shape[1]
    rim = rim_index.shape[1]
    rim_from = node_rows + n_lon * halo
    rim_to = rim_from + 2 * rim
    chunks = edges.shape[0] // CHUNK
    blocks = CHUNK // LANES

    barrier = pltpu.get_barrier_semaphore()
    for d in range(1, n_lon):
        pl.semaphore_signal(
            barrier, inc=1, device_id=(a, lax.rem(b + d, n_lon)), device_id_type=MESH
        )

    @pl.when(a > 0)
    def _():
        pl.semaphore_signal(barrier, inc=1, device_id=(a - 1, b), device_id_type=MESH)

    @pl.when(a < n_lat - 1)
    def _():
        pl.semaphore_signal(barrier, inc=1, device_id=(a + 1, b), device_id_type=MESH)

    sender_rows = pl.ds(width, width)
    pairs = [
        (rim_index_in, rim_index),
        (nodes_in, nodes),
        (w1_in.at[sender_rows], w1.at[sender_rows]),
        (send_index_in, send_index),
        (senders_in, senders),
        (receivers_in, receivers),
        (w1_in.at[pl.ds(0, width)], w1.at[pl.ds(0, width)]),
        (w1_in.at[pl.ds(2 * width, width)], w1.at[pl.ds(2 * width, width)]),
        (b1_in, b1),
        (edges_in, edges),
        (c1_in, c1),
        (w2_in, w2),
        (v2_in, v2),
        (gain_in, gain),
        (ngain_in, ngain),
        (v1_in, v1),
    ]
    loads = [
        pltpu.make_async_copy(src, dst, load_sem.at[i]) for i, (src, dst) in enumerate(pairs)
    ]
    for copy in loads:
        copy.start()

    @pl.when(a == 0)
    def _():
        rims_far[:rim] = jnp.zeros((rim, width), BF16)

    @pl.when(a == n_lat - 1)
    def _():
        rims_far[rim:] = jnp.zeros((rim, width), BF16)

    for copy in loads[:4]:
        copy.wait()
    lists = jnp.concatenate(
        [send_index[...], jnp.zeros((n_lon, LANES - halo), jnp.int32)], axis=1
    )
    list_turned = turned(jnp.concatenate([rim_index[...], lists], axis=0))
    own = nodes[...]
    by_sender = (0.5 * dot(own, w1[sender_rows])).astype(BF16)
    chosen = [pick_rows(list_turned[:, side : side + 1], 0, node_rows) for side in range(2)]
    outgoing[: 2 * rim] = dot(jnp.concatenate(chosen, axis=0), by_sender).astype(BF16)

    below = jnp.where(a > 0, 1, 0)
    above = jnp.where(a < n_lat - 1, 1, 0)
    pl.semaphore_wait(barrier, n_lon - 1 + below + above)
    rims = [
        pltpu.make_async_remote_copy(
            src_ref=outgoing.at[pl.ds(side * rim, rim)],
            dst_ref=rims_far.at[pl.ds(side * rim, rim)],
            send_sem=send_sem.at[n_lon - 1 + side],
            recv_sem=recv_sem.at[n_lon - 1 + side],
            device_id=(a + 1 - 2 * side, b),
            device_id_type=MESH,
        )
        for side in range(2)
    ]

    @pl.when(a < n_lat - 1)
    def _():
        rims[0].start()

    @pl.when(a > 0)
    def _():
        rims[1].start()

    chosen = [
        pick_rows(list_turned[:halo, 2 + p : 3 + p], 0, node_rows) for p in range(n_lon)
    ]
    outgoing[2 * rim :] = dot(jnp.concatenate(chosen, axis=0), by_sender).astype(BF16)
    mine = pl.multiple_of(b * halo, halo)
    band = []
    for d in range(1, n_lon):
        p = lax.rem(b + d, n_lon)
        copy = pltpu.make_async_remote_copy(
            src_ref=outgoing.at[pl.ds(2 * rim + pl.multiple_of(p * halo, halo), halo)],
            dst_ref=band_far.at[pl.ds(mine, halo)],
            send_sem=send_sem.at[d - 1],
            recv_sem=recv_sem.at[d - 1],
            device_id=(a, p),
            device_id_type=MESH,
        )
        copy.start()
        band.append(copy)
    band_far[pl.ds(mine, halo)] = outgoing[pl.ds(2 * rim + mine, halo)]

    for copy in loads[4:]:
        copy.wait()
    sender_turned = turned(senders[...])
    receiver_turned = turned(receivers[...])
    by_receiver = (0.5 * (dot(own, w1[2 * width :]) + b1[...])).astype(BF16)
    near = jnp.concatenate(
        [(0.5 * w1[:width].astype(F32)).astype(BF16), by_receiver, by_sender], axis=0
    )

    def marks(turned_rows, i, low, high):
        rows = [
            pick_rows(turned_rows[:, j : j + 1], low, high)
            for j in range(i * blocks, (i + 1) * blocks)
        ]
        return jnp.concatenate(rows, axis=0)

    def near_part(i):
        span = slice(i * CHUNK, (i + 1) * CHUNK)
        marks_far[span] = marks(sender_turned, i, rim_from, rim_to)
        row = [
            mark(jnp.broadcast_to(receivers[j : j + 1], ids.shape).astype(jnp.int16) == ids)
            for j in range(i * blocks, (i + 1) * blocks)
        ]
        member[:, span] = jnp.concatenate(row, axis=1)
        rows = [
            edges[span],
            marks(receiver_turned, i, 0, node_rows),
            marks(sender_turned, i, 0, node_rows),
        ]
        return rows

    ids = row_ids(node_rows)
    ahead = min(AHEAD, chunks)
    for i in range(ahead):
        pre[i * CHUNK : (i + 1) * CHUNK] = dot(jnp.concatenate(near_part(i), axis=1), near)
    w2c[...] = centred_weights(w2[...])
    v2c[...] = centred_weights(v2[...])
    node_pre[...] = 0.5 * (dot(own, v1[:width]) + c1[...])

    for copy in band:
        copy.wait()
    from_band = band_far[...]
    for i in range(ahead):
        pre[i * CHUNK : (i + 1) * CHUNK] += dot(
            marks(sender_turned, i, node_rows, rim_from), from_band
        )
    wide = jnp.concatenate([near, from_band], axis=0)
    for i in range(ahead, chunks):
        rows = near_part(i) + [marks(sender_turned, i, node_rows, rim_from)]
        pre[i * CHUNK : (i + 1) * CHUNK] = dot(jnp.concatenate(rows, axis=1), wide)

    @pl.when(a < n_lat - 1)
    def _():
        rims[0].wait_send()
        rims[1].wait_recv()

    @pl.when(a > 0)
    def _():
        rims[1].wait_send()
        rims[0].wait_recv()


def finish(
    count,
    rims_far,
    marks_far,
    member,
    pre,
    node_pre,
    w2c,
    v2c,
    nodes,
    gain,
    ngain,
    v1,
    edges,
    new_nodes,
    new_edges,
    fresh,
    fresh_nodes,
    store_sem,
):
    node_rows, width = nodes.shape
    chunks = edges.shape[0] // CHUNK
    ones = jnp.full((width, LANES), 1.0 / width, BF16)
    live = count[0]
    messages = jnp.zeros((node_rows, width), F32)
    for i in range(chunks):
        span = slice(i * CHUNK, (i + 1) * CHUNK)
        hidden = halved_silu(pre[span] + dot(marks_far[span], rims_far[...]))
        y = dot(hidden, w2c[...])
        scale = inverse_spread(y, ones)
        slot = lax.broadcasted_iota(jnp.int32, scale.shape, 0) + i * CHUNK
        scale = jnp.where(slot < live, scale, 0.0)
        scale = jnp.concatenate([scale] * (width // LANES), axis=1)
        update = (y * scale * gain[...]).astype(BF16)
        fresh[span] = edges[span] + update
        messages = messages + dot(member[:, span], update)

    edge_store = pltpu.make_async_copy(fresh, new_edges, store_sem.at[0])
    edge_store.start()
    h = node_pre[...] + 0.5 * dot(messages.astype(BF16), v1[width:])
    z = dot(halved_silu(h), v2c[...])
    scale = inverse_spread(z, ones)
    scale = jnp.concatenate([scale] * (width // LANES), axis=1)
    fresh_nodes[...] = (nodes[...].astype(F32) + z * scale * ngain[...]).astype(BF16)
    node_store = pltpu.make_async_copy(fresh_nodes, new_nodes, store_sem.at[1])
    node_store.start()
    edge_store.wait()
    node_store.wait()


def in_hbm(x):
    return pltpu.with_memory_space_constraint(x, pltpu.HBM)


def local(
    n_lat,
    n_lon,
    nodes,
    edges,
    senders,
    receivers,
    edge_count,
    send_index,
    rim_index,
    edge_w1,
    edge_b1,
    edge_w2,
    edge_gain,
    node_w1,
    node_b1,
    node_w2,
    node_gain,
):
    width = nodes.shape[1]
    inner = (
        rim_index,
        nodes,
        edge_w1,
        send_index,
        senders.reshape(-1, LANES),
        edge_b1.reshape(1, width),
        node_b1.reshape(1, width),
        edge_w2,
        node_w2,
        receivers.reshape(-1, LANES),
    )
    passed = (
        edge_gain.reshape(1, width),
        node_gain.reshape(1, width),
        node_w1,
        edges,
    )
    operands = [in_hbm(x) for x in inner + passed]
    node_rows, edge_rows = nodes.shape[0], edges.shape[0]
    band_rows, rim_rows = n_lon * send_index.shape[1], 2 * rim_index.shape[1]
    handed = [
        ((rim_rows, width), BF16),
        ((edge_rows, rim_rows), BF16),
        ((node_rows, edge_rows), BF16),
        (edges.shape, F32),
        (nodes.shape, F32),
        (edge_w2.shape, BF16),
        (node_w2.shape, BF16),
        (nodes.shape, BF16),
    ] + [(x.shape, x.dtype) for x in passed]
    scratch = [x for x in inner if x is not nodes]
    hbm = pl.BlockSpec(memory_space=pltpu.HBM)
    vmem = pl.BlockSpec(memory_space=pltpu.VMEM)
    limit = 24 * 1024 * 1024
    between = pl.pallas_call(
        functools.partial(exchange, n_lat, n_lon),
        out_shape=tuple(pltpu.VMEM(shape, dtype) for shape, dtype in handed),
        in_specs=[hbm] * len(operands),
        out_specs=(vmem,) * len(handed),
        scratch_shapes=[pltpu.VMEM(x.shape, x.dtype) for x in scratch]
        + [
            pltpu.VMEM((band_rows, width), BF16),
            pltpu.VMEM((rim_rows + band_rows, width), BF16),
            pltpu.SemaphoreType.DMA((len(operands) + 2,)),
            pltpu.SemaphoreType.DMA((n_lon + 1,)),
            pltpu.SemaphoreType.DMA((n_lon + 1,)),
        ],
        compiler_params=pltpu.CompilerParams(
            collective_id=0, has_side_effects=True, vmem_limit_bytes=limit
        ),
    )(*operands)
    return pl.pallas_call(
        finish,
        out_shape=(pltpu.HBM(nodes.shape, BF16), pltpu.HBM(edges.shape, BF16)),
        in_specs=[pl.BlockSpec(memory_space=pltpu.SMEM)] + [vmem] * len(handed),
        out_specs=(hbm, hbm),
        scratch_shapes=[
            pltpu.VMEM(edges.shape, BF16),
            pltpu.VMEM(nodes.shape, BF16),
            pltpu.SemaphoreType.DMA((2,)),
        ],
        compiler_params=pltpu.CompilerParams(vmem_limit_bytes=limit),
    )(edge_count, *between)


def solution(mesh):
    rows, flat = P(("lat", "lon"), None), P(("lat", "lon"))
    return jax.shard_map(
        functools.partial(local, mesh.shape["lat"], mesh.shape["lon"]),
        mesh=mesh,
        in_specs=(rows, rows, flat, flat, flat, rows, rows) + (P(),) * 8,
        out_specs=(rows, rows),
        check_vma=False,
    )
```

```python
import functools

import jax
import jax.numpy as jnp
from jax import lax
from jax.experimental import pallas as pl
from jax.experimental.pallas import tpu as pltpu
from jax.sharding import PartitionSpec as P

BF16 = jnp.bfloat16
F32 = jnp.float32
MESH = pl.DeviceIdType.MESH
LANES = 128
CHUNK = 512
STEP = 1024


def dot(a, b):
    return jnp.dot(a, b, preferred_element_type=F32)


def lane_ids(rows):
    return lax.broadcasted_iota(jnp.int32, (rows, LANES), 1).astype(jnp.int16)


def row_ids(rows):
    return lax.broadcasted_iota(jnp.int32, (rows, LANES), 0).astype(jnp.int16)


def mark(hit):
    return jnp.where(hit, jnp.ones(hit.shape, BF16), jnp.zeros(hit.shape, BF16))


def pick_rows(columns, low, high):
    n = columns.shape[0]
    spread = jnp.broadcast_to(columns, (n, LANES)).astype(jnp.int16)
    lanes = lane_ids(n)
    tiles = [mark(spread == lanes + jnp.int16(t)) for t in range(low, high, LANES)]
    return jnp.concatenate(tiles, axis=1)


def turned(block):
    short = LANES - block.shape[0]
    if short:
        block = jnp.concatenate([block, jnp.zeros((short, LANES), jnp.int32)], axis=0)
    return jnp.transpose(block)


def centred_weights(w):
    w = w.astype(F32)
    return (w - jnp.mean(w, axis=-1, keepdims=True)).astype(BF16)


def halved_silu(h):
    return (h + h * jnp.tanh(h)).astype(BF16)


def inverse_spread(y, ones):
    return lax.rsqrt(dot((y * y).astype(BF16), ones) + 1e-05)


def exchange(
    n_lat,
    n_lon,
    rim_index_in,
    nodes_in,
    w1_in,
    send_index_in,
    senders_in,
    b1_in,
    c1_in,
    w2_in,
    v2_in,
    receivers_in,
    gain_in,
    ngain_in,
    v1_in,
    edges_in,
    far,
    marks_far,
    member,
    pre,
    node_pre,
    w2c,
    v2c,
    nodes,
    gain,
    ngain,
    v1,
    edges,
    rim_index,
    w1,
    send_index,
    senders,
    b1,
    c1,
    w2,
    v2,
    receivers,
    outgoing,
    load_sem,
    send_sem,
    recv_sem,
):
    a, b = lax.axis_index("lat"), lax.axis_index("lon")
    node_rows, width = nodes.shape
    halo = send_index.shape[1]
    rim = rim_index.shape[1]
    halos = n_lon * halo
    table_rows = node_rows + halos + 2 * rim
    chunks = edges.shape[0] // CHUNK
    blocks = CHUNK // LANES

    barrier = pltpu.get_barrier_semaphore()
    for d in range(1, n_lon):
        pl.semaphore_signal(
            barrier, inc=1, device_id=(a, lax.rem(b + d, n_lon)), device_id_type=MESH
        )

    @pl.when(a > 0)
    def _():
        pl.semaphore_signal(barrier, inc=1, device_id=(a - 1, b), device_id_type=MESH)

    @pl.when(a < n_lat - 1)
    def _():
        pl.semaphore_signal(barrier, inc=1, device_id=(a + 1, b), device_id_type=MESH)

    sender_rows = pl.ds(width, width)
    pairs = [
        (rim_index_in, rim_index),
        (nodes_in, nodes),
        (w1_in.at[sender_rows], w1.at[sender_rows]),
        (send_index_in, send_index),
        (senders_in, senders),
        (receivers_in, receivers),
        (w1_in.at[pl.ds(0, width)], w1.at[pl.ds(0, width)]),
        (w1_in.at[pl.ds(2 * width, width)], w1.at[pl.ds(2 * width, width)]),
        (b1_in, b1),
        (edges_in, edges),
        (c1_in, c1),
        (w2_in, w2),
        (v2_in, v2),
        (gain_in, gain),
        (ngain_in, ngain),
        (v1_in, v1),
    ]
    loads = [
        pltpu.make_async_copy(src, dst, load_sem.at[i]) for i, (src, dst) in enumerate(pairs)
    ]
    for copy in loads:
        copy.start()

    @pl.when(a == 0)
    def _():
        far[halos : halos + rim] = jnp.zeros((rim, width), BF16)

    @pl.when(a == n_lat - 1)
    def _():
        far[halos + rim :] = jnp.zeros((rim, width), BF16)

    for copy in loads[:4]:
        copy.wait()
    lists = jnp.concatenate(
        [send_index[...], jnp.zeros((n_lon, LANES - halo), jnp.int32)], axis=1
    )
    list_turned = turned(jnp.concatenate([rim_index[...], lists], axis=0))
    own = nodes[...]
    by_sender = (0.5 * dot(own, w1[sender_rows])).astype(BF16)
    chosen = [pick_rows(list_turned[:, side : side + 1], 0, node_rows) for side in range(2)]
    outgoing[: 2 * rim] = dot(jnp.concatenate(chosen, axis=0), by_sender).astype(BF16)

    below = jnp.where(a > 0, 1, 0)
    above = jnp.where(a < n_lat - 1, 1, 0)
    pl.semaphore_wait(barrier, n_lon - 1 + below + above)
    rims = [
        pltpu.make_async_remote_copy(
            src_ref=outgoing.at[pl.ds(side * rim, rim)],
            dst_ref=far.at[pl.ds(halos + side * rim, rim)],
            send_sem=send_sem.at[n_lon - 1 + side],
            recv_sem=recv_sem.at[n_lon - 1 + side],
            device_id=(a + 1 - 2 * side, b),
            device_id_type=MESH,
        )
        for side in range(2)
    ]

    @pl.when(a < n_lat - 1)
    def _():
        rims[0].start()

    @pl.when(a > 0)
    def _():
        rims[1].start()

    chosen = [
        pick_rows(list_turned[:halo, 2 + p : 3 + p], 0, node_rows) for p in range(n_lon)
    ]
    outgoing[2 * rim :] = dot(jnp.concatenate(chosen, axis=0), by_sender).astype(BF16)
    mine = pl.multiple_of(b * halo, halo)
    band = []
    for d in range(1, n_lon):
        p = lax.rem(b + d, n_lon)
        copy = pltpu.make_async_remote_copy(
            src_ref=outgoing.at[pl.ds(2 * rim + pl.multiple_of(p * halo, halo), halo)],
            dst_ref=far.at[pl.ds(mine, halo)],
            send_sem=send_sem.at[d - 1],
            recv_sem=recv_sem.at[d - 1],
            device_id=(a, p),
            device_id_type=MESH,
        )
        copy.start()
        band.append(copy)
    far[pl.ds(mine, halo)] = outgoing[pl.ds(2 * rim + mine, halo)]

    for copy in loads[4:]:
        copy.wait()
    sender_turned = turned(senders[...])
    receiver_turned = turned(receivers[...])
    by_receiver = (0.5 * (dot(own, w1[2 * width :]) + b1[...])).astype(BF16)
    near = jnp.concatenate(
        [(0.5 * w1[:width].astype(F32)).astype(BF16), by_receiver, by_sender], axis=0
    )

    def marks(turned_rows, i, low, high):
        rows = [
            pick_rows(turned_rows[:, j : j + 1], low, high)
            for j in range(i * blocks, (i + 1) * blocks)
        ]
        return jnp.concatenate(rows, axis=0)

    def near_part(i):
        span = slice(i * CHUNK, (i + 1) * CHUNK)
        marks_far[span] = marks(sender_turned, i, node_rows, table_rows)
        row = [
            mark(jnp.broadcast_to(receivers[j : j + 1], ids.shape).astype(jnp.int16) == ids)
            for j in range(i * blocks, (i + 1) * blocks)
        ]
        member[:, span] = jnp.concatenate(row, axis=1)
        rows = [
            edges[span],
            marks(receiver_turned, i, 0, node_rows),
            marks(sender_turned, i, 0, node_rows),
        ]
        return rows

    ids = row_ids(node_rows)
    for i in range(chunks):
        pre[i * CHUNK : (i + 1) * CHUNK] = dot(jnp.concatenate(near_part(i), axis=1), near)
    w2c[...] = centred_weights(w2[...])
    v2c[...] = centred_weights(v2[...])
    node_pre[...] = 0.5 * (dot(own, v1[:width]) + c1[...])

    for copy in band:
        copy.wait()

    @pl.when(a < n_lat - 1)
    def _():
        rims[0].wait_send()
        rims[1].wait_recv()

    @pl.when(a > 0)
    def _():
        rims[1].wait_send()
        rims[0].wait_recv()


def finish(
    count,
    far,
    marks_far,
    member,
    pre,
    node_pre,
    w2c,
    v2c,
    nodes,
    gain,
    ngain,
    v1,
    edges,
    new_nodes,
    new_edges,
    fresh,
    fresh_nodes,
    store_sem,
):
    node_rows, width = nodes.shape
    chunks = edges.shape[0] // STEP
    ones = jnp.full((width, LANES), 1.0 / width, BF16)
    live = count[0]
    messages = jnp.zeros((node_rows, width), F32)
    for i in range(chunks):
        span = slice(i * STEP, (i + 1) * STEP)
        hidden = halved_silu(pre[span] + dot(marks_far[span], far[...]))
        y = dot(hidden, w2c[...])
        scale = inverse_spread(y, ones)
        slot = lax.broadcasted_iota(jnp.int32, scale.shape, 0) + i * STEP
        scale = jnp.where(slot < live, scale, 0.0)
        scale = jnp.concatenate([scale] * (width // LANES), axis=1)
        update = (y * scale * gain[...]).astype(BF16)
        fresh[span] = edges[span] + update
        messages = messages + dot(member[:, span], update)

    edge_store = pltpu.make_async_copy(fresh, new_edges, store_sem.at[0])
    edge_store.start()
    h = node_pre[...] + 0.5 * dot(messages.astype(BF16), v1[width:])
    z = dot(halved_silu(h), v2c[...])
    scale = inverse_spread(z, ones)
    scale = jnp.concatenate([scale] * (width // LANES), axis=1)
    fresh_nodes[...] = (nodes[...].astype(F32) + z * scale * ngain[...]).astype(BF16)
    node_store = pltpu.make_async_copy(fresh_nodes, new_nodes, store_sem.at[1])
    node_store.start()
    edge_store.wait()
    node_store.wait()


def in_hbm(x):
    return pltpu.with_memory_space_constraint(x, pltpu.HBM)


def local(
    n_lat,
    n_lon,
    nodes,
    edges,
    senders,
    receivers,
    edge_count,
    send_index,
    rim_index,
    edge_w1,
    edge_b1,
    edge_w2,
    edge_gain,
    node_w1,
    node_b1,
    node_w2,
    node_gain,
):
    width = nodes.shape[1]
    inner = (
        rim_index,
        nodes,
        edge_w1,
        send_index,
        senders.reshape(-1, LANES),
        edge_b1.reshape(1, width),
        node_b1.reshape(1, width),
        edge_w2,
        node_w2,
        receivers.reshape(-1, LANES),
    )
    passed = (
        edge_gain.reshape(1, width),
        node_gain.reshape(1, width),
        node_w1,
        edges,
    )
    operands = [in_hbm(x) for x in inner + passed]
    node_rows, edge_rows = nodes.shape[0], edges.shape[0]
    listed = n_lon * send_index.shape[1] + 2 * rim_index.shape[1]
    handed = [
        ((listed, width), BF16),
        ((edge_rows, listed), BF16),
        ((node_rows, edge_rows), BF16),
        (edges.shape, F32),
        (nodes.shape, F32),
        (edge_w2.shape, BF16),
        (node_w2.shape, BF16),
        (nodes.shape, BF16),
    ] + [(x.shape, x.dtype) for x in passed]
    scratch = [x for x in inner if x is not nodes]
    hbm = pl.BlockSpec(memory_space=pltpu.HBM)
    vmem = pl.BlockSpec(memory_space=pltpu.VMEM)
    limit = 24 * 1024 * 1024
    between = pl.pallas_call(
        functools.partial(exchange, n_lat, n_lon),
        out_shape=tuple(pltpu.VMEM(shape, dtype) for shape, dtype in handed),
        in_specs=[hbm] * len(operands),
        out_specs=(vmem,) * len(handed),
        scratch_shapes=[pltpu.VMEM(x.shape, x.dtype) for x in scratch]
        + [
            pltpu.VMEM((listed, width), BF16),
            pltpu.SemaphoreType.DMA((len(operands) + 2,)),
            pltpu.SemaphoreType.DMA((n_lon + 1,)),
            pltpu.SemaphoreType.DMA((n_lon + 1,)),
        ],
        compiler_params=pltpu.CompilerParams(
            collective_id=0, has_side_effects=True, vmem_limit_bytes=limit
        ),
    )(*operands)
    return pl.pallas_call(
        finish,
        out_shape=(pltpu.HBM(nodes.shape, BF16), pltpu.HBM(edges.shape, BF16)),
        in_specs=[pl.BlockSpec(memory_space=pltpu.SMEM)] + [vmem] * len(handed),
        out_specs=(hbm, hbm),
        scratch_shapes=[
            pltpu.VMEM(edges.shape, BF16),
            pltpu.VMEM(nodes.shape, BF16),
            pltpu.SemaphoreType.DMA((2,)),
        ],
        compiler_params=pltpu.CompilerParams(vmem_limit_bytes=limit),
    )(edge_count, *between)


def solution(mesh):
    rows, flat = P(("lat", "lon"), None), P(("lat", "lon"))
    return jax.shard_map(
        functools.partial(local, mesh.shape["lat"], mesh.shape["lon"]),
        mesh=mesh,
        in_specs=(rows, rows, flat, flat, flat, rows, rows) + (P(),) * 8,
        out_specs=(rows, rows),
        check_vma=False,
    )
```

```python
import functools

import jax
import jax.numpy as jnp
from jax import lax
from jax.experimental import pallas as pl
from jax.experimental.pallas import tpu as pltpu
from jax.sharding import PartitionSpec as P

BF16 = jnp.bfloat16
F32 = jnp.float32
MESH = pl.DeviceIdType.MESH
LANES = 128
CHUNK = 512
STEP = 1536


def dot(a, b):
    return jnp.dot(a, b, preferred_element_type=F32)


def lane_ids(rows):
    return lax.broadcasted_iota(jnp.int32, (rows, LANES), 1).astype(jnp.int16)


def row_ids(rows):
    return lax.broadcasted_iota(jnp.int32, (rows, LANES), 0).astype(jnp.int16)


def mark(hit):
    return jnp.where(hit, jnp.ones(hit.shape, BF16), jnp.zeros(hit.shape, BF16))


def pick_rows(columns, low, high):
    n = columns.shape[0]
    spread = jnp.broadcast_to(columns, (n, LANES)).astype(jnp.int16)
    lanes = lane_ids(n)
    tiles = [mark(spread == lanes + jnp.int16(t)) for t in range(low, high, LANES)]
    return jnp.concatenate(tiles, axis=1)


def turned(block):
    short = LANES - block.shape[0]
    if short:
        block = jnp.concatenate([block, jnp.zeros((short, LANES), jnp.int32)], axis=0)
    return jnp.transpose(block)


def centred_weights(w):
    w = w.astype(F32)
    return (w - jnp.mean(w, axis=-1, keepdims=True)).astype(BF16)


def halved_silu(h):
    return (h + h * jnp.tanh(h)).astype(BF16)


def inverse_spread(y, ones):
    return lax.rsqrt(dot((y * y).astype(BF16), ones) + 1e-05)


def exchange(
    n_lat,
    n_lon,
    rim_index_in,
    nodes_in,
    w1_in,
    send_index_in,
    senders_in,
    b1_in,
    c1_in,
    w2_in,
    v2_in,
    receivers_in,
    gain_in,
    ngain_in,
    v1_in,
    edges_in,
    far,
    marks_far,
    member,
    pre,
    node_pre,
    w2c,
    v2c,
    nodes,
    gain,
    ngain,
    v1,
    edges,
    rim_index,
    w1,
    send_index,
    senders,
    b1,
    c1,
    w2,
    v2,
    receivers,
    outgoing,
    load_sem,
    send_sem,
    recv_sem,
):
    a, b = lax.axis_index("lat"), lax.axis_index("lon")
    node_rows, width = nodes.shape
    halo = send_index.shape[1]
    rim = rim_index.shape[1]
    halos = n_lon * halo
    table_rows = node_rows + halos + 2 * rim
    chunks = edges.shape[0] // CHUNK
    blocks = CHUNK // LANES

    sender_rows = pl.ds(width, width)
    pairs = [
        (rim_index_in, rim_index),
        (nodes_in, nodes),
        (w1_in.at[sender_rows], w1.at[sender_rows]),
        (send_index_in, send_index),
        (senders_in, senders),
        (receivers_in, receivers),
        (w1_in.at[pl.ds(0, width)], w1.at[pl.ds(0, width)]),
        (w1_in.at[pl.ds(2 * width, width)], w1.at[pl.ds(2 * width, width)]),
        (b1_in, b1),
        (edges_in, edges),
        (c1_in, c1),
        (w2_in, w2),
        (v2_in, v2),
        (gain_in, gain),
        (ngain_in, ngain),
        (v1_in, v1),
    ]
    loads = [
        pltpu.make_async_copy(src, dst, load_sem.at[i]) for i, (src, dst) in enumerate(pairs)
    ]
    for copy in loads[:4]:
        copy.start()

    barrier = pltpu.get_barrier_semaphore()
    for d in range(1, n_lon):
        pl.semaphore_signal(
            barrier, inc=1, device_id=(a, lax.rem(b + d, n_lon)), device_id_type=MESH
        )

    @pl.when(a > 0)
    def _():
        pl.semaphore_signal(barrier, inc=1, device_id=(a - 1, b), device_id_type=MESH)

    @pl.when(a < n_lat - 1)
    def _():
        pl.semaphore_signal(barrier, inc=1, device_id=(a + 1, b), device_id_type=MESH)

    for copy in loads[4:]:
        copy.start()

    @pl.when(a == 0)
    def _():
        far[halos : halos + rim] = jnp.zeros((rim, width), BF16)

    @pl.when(a == n_lat - 1)
    def _():
        far[halos + rim :] = jnp.zeros((rim, width), BF16)

    for copy in loads[:4]:
        copy.wait()
    lists = jnp.concatenate(
        [send_index[...], jnp.zeros((n_lon, LANES - halo), jnp.int32)], axis=1
    )
    list_turned = turned(jnp.concatenate([rim_index[...], lists], axis=0))
    own = nodes[...]
    by_sender = (0.5 * dot(own, w1[sender_rows])).astype(BF16)
    chosen = [pick_rows(list_turned[:, side : side + 1], 0, node_rows) for side in range(2)]
    outgoing[: 2 * rim] = dot(jnp.concatenate(chosen, axis=0), by_sender).astype(BF16)

    below = jnp.where(a > 0, 1, 0)
    above = jnp.where(a < n_lat - 1, 1, 0)
    pl.semaphore_wait(barrier, n_lon - 1 + below + above)
    rims = [
        pltpu.make_async_remote_copy(
            src_ref=outgoing.at[pl.ds(side * rim, rim)],
            dst_ref=far.at[pl.ds(halos + side * rim, rim)],
            send_sem=send_sem.at[n_lon - 1 + side],
            recv_sem=recv_sem.at[n_lon - 1 + side],
            device_id=(a + 1 - 2 * side, b),
            device_id_type=MESH,
        )
        for side in range(2)
    ]

    @pl.when(a < n_lat - 1)
    def _():
        rims[0].start()

    @pl.when(a > 0)
    def _():
        rims[1].start()

    chosen = [
        pick_rows(list_turned[:halo, 2 + p : 3 + p], 0, node_rows) for p in range(n_lon)
    ]
    outgoing[2 * rim :] = dot(jnp.concatenate(chosen, axis=0), by_sender).astype(BF16)
    mine = pl.multiple_of(b * halo, halo)
    band = []
    for d in range(1, n_lon):
        p = lax.rem(b + d, n_lon)
        copy = pltpu.make_async_remote_copy(
            src_ref=outgoing.at[pl.ds(2 * rim + pl.multiple_of(p * halo, halo), halo)],
            dst_ref=far.at[pl.ds(mine, halo)],
            send_sem=send_sem.at[d - 1],
            recv_sem=recv_sem.at[d - 1],
            device_id=(a, p),
            device_id_type=MESH,
        )
        copy.start()
        band.append(copy)
    far[pl.ds(mine, halo)] = outgoing[pl.ds(2 * rim + mine, halo)]

    for copy in loads[4:]:
        copy.wait()
    sender_turned = turned(senders[...])
    receiver_turned = turned(receivers[...])
    by_receiver = (0.5 * (dot(own, w1[2 * width :]) + b1[...])).astype(BF16)
    near = jnp.concatenate(
        [(0.5 * w1[:width].astype(F32)).astype(BF16), by_receiver, by_sender], axis=0
    )

    def marks(turned_rows, i, low, high):
        rows = [
            pick_rows(turned_rows[:, j : j + 1], low, high)
            for j in range(i * blocks, (i + 1) * blocks)
        ]
        return jnp.concatenate(rows, axis=0)

    def near_part(i):
        span = slice(i * CHUNK, (i + 1) * CHUNK)
        marks_far[span] = marks(sender_turned, i, node_rows, table_rows)
        row = [
            mark(jnp.broadcast_to(receivers[j : j + 1], ids.shape).astype(jnp.int16) == ids)
            for j in range(i * blocks, (i + 1) * blocks)
        ]
        member[:, span] = jnp.concatenate(row, axis=1)
        rows = [
            edges[span],
            marks(receiver_turned, i, 0, node_rows),
            marks(sender_turned, i, 0, node_rows),
        ]
        return rows

    ids = row_ids(node_rows)
    for i in range(chunks):
        pre[i * CHUNK : (i + 1) * CHUNK] = dot(jnp.concatenate(near_part(i), axis=1), near)
    w2c[...] = centred_weights(w2[...])
    v2c[...] = centred_weights(v2[...])
    node_pre[...] = 0.5 * (dot(own, v1[:width]) + c1[...])

    for copy in band:
        copy.wait()

    @pl.when(a < n_lat - 1)
    def _():
        rims[0].wait_send()
        rims[1].wait_recv()

    @pl.when(a > 0)
    def _():
        rims[1].wait_send()
        rims[0].wait_recv()


def finish(
    count,
    far,
    marks_far,
    member,
    pre,
    node_pre,
    w2c,
    v2c,
    nodes,
    gain,
    ngain,
    v1,
    edges,
    new_nodes,
    new_edges,
    fresh,
    fresh_nodes,
    store_sem,
):
    node_rows, width = nodes.shape
    chunks = edges.shape[0] // STEP
    ones = jnp.full((width, LANES), 1.0 / width, BF16)
    live = count[0]
    messages = jnp.zeros((node_rows, width), F32)
    for i in range(chunks):
        span = slice(i * STEP, (i + 1) * STEP)
        hidden = halved_silu(pre[span] + dot(marks_far[span], far[...]))
        y = dot(hidden, w2c[...])
        scale = inverse_spread(y, ones)
        slot = lax.broadcasted_iota(jnp.int32, scale.shape, 0) + i * STEP
        scale = jnp.where(slot < live, scale, 0.0)
        scale = jnp.concatenate([scale] * (width // LANES), axis=1)
        update = (y * scale * gain[...]).astype(BF16)
        fresh[span] = edges[span] + update
        messages = messages + dot(member[:, span], update)

    edge_store = pltpu.make_async_copy(fresh, new_edges, store_sem.at[0])
    edge_store.start()
    h = node_pre[...] + 0.5 * dot(messages.astype(BF16), v1[width:])
    z = dot(halved_silu(h), v2c[...])
    scale = inverse_spread(z, ones)
    scale = jnp.concatenate([scale] * (width // LANES), axis=1)
    fresh_nodes[...] = (nodes[...].astype(F32) + z * scale * ngain[...]).astype(BF16)
    node_store = pltpu.make_async_copy(fresh_nodes, new_nodes, store_sem.at[1])
    node_store.start()
    edge_store.wait()
    node_store.wait()


def in_hbm(x):
    return pltpu.with_memory_space_constraint(x, pltpu.HBM)


def local(
    n_lat,
    n_lon,
    nodes,
    edges,
    senders,
    receivers,
    edge_count,
    send_index,
    rim_index,
    edge_w1,
    edge_b1,
    edge_w2,
    edge_gain,
    node_w1,
    node_b1,
    node_w2,
    node_gain,
):
    width = nodes.shape[1]
    inner = (
        rim_index,
        nodes,
        edge_w1,
        send_index,
        senders.reshape(-1, LANES),
        edge_b1.reshape(1, width),
        node_b1.reshape(1, width),
        edge_w2,
        node_w2,
        receivers.reshape(-1, LANES),
    )
    passed = (
        edge_gain.reshape(1, width),
        node_gain.reshape(1, width),
        node_w1,
        edges,
    )
    operands = [in_hbm(x) for x in inner + passed]
    node_rows, edge_rows = nodes.shape[0], edges.shape[0]
    listed = n_lon * send_index.shape[1] + 2 * rim_index.shape[1]
    handed = [
        ((listed, width), BF16),
        ((edge_rows, listed), BF16),
        ((node_rows, edge_rows), BF16),
        (edges.shape, F32),
        (nodes.shape, F32),
        (edge_w2.shape, BF16),
        (node_w2.shape, BF16),
        (nodes.shape, BF16),
    ] + [(x.shape, x.dtype) for x in passed]
    scratch = [x for x in inner if x is not nodes]
    hbm = pl.BlockSpec(memory_space=pltpu.HBM)
    vmem = pl.BlockSpec(memory_space=pltpu.VMEM)
    limit = 24 * 1024 * 1024
    between = pl.pallas_call(
        functools.partial(exchange, n_lat, n_lon),
        out_shape=tuple(pltpu.VMEM(shape, dtype) for shape, dtype in handed),
        in_specs=[hbm] * len(operands),
        out_specs=(vmem,) * len(handed),
        scratch_shapes=[pltpu.VMEM(x.shape, x.dtype) for x in scratch]
        + [
            pltpu.VMEM((listed, width), BF16),
            pltpu.SemaphoreType.DMA((len(operands) + 2,)),
            pltpu.SemaphoreType.DMA((n_lon + 1,)),
            pltpu.SemaphoreType.DMA((n_lon + 1,)),
        ],
        compiler_params=pltpu.CompilerParams(
            collective_id=0, has_side_effects=True, vmem_limit_bytes=limit
        ),
    )(*operands)
    return pl.pallas_call(
        finish,
        out_shape=(pltpu.HBM(nodes.shape, BF16), pltpu.HBM(edges.shape, BF16)),
        in_specs=[pl.BlockSpec(memory_space=pltpu.SMEM)] + [vmem] * len(handed),
        out_specs=(hbm, hbm),
        scratch_shapes=[
            pltpu.VMEM(edges.shape, BF16),
            pltpu.VMEM(nodes.shape, BF16),
            pltpu.SemaphoreType.DMA((2,)),
        ],
        compiler_params=pltpu.CompilerParams(vmem_limit_bytes=limit),
    )(edge_count, *between)


def solution(mesh):
    rows, flat = P(("lat", "lon"), None), P(("lat", "lon"))
    return jax.shard_map(
        functools.partial(local, mesh.shape["lat"], mesh.shape["lon"]),
        mesh=mesh,
        in_specs=(rows, rows, flat, flat, flat, rows, rows) + (P(),) * 8,
        out_specs=(rows, rows),
        check_vma=False,
    )
```
